128 devices in a mesh: slide: 8 (over x, z_hi), seq: 16 (over y, z_lo, core).
Axes of the slice: x: 4, y: 4, z: 4 (z_hi: 2, z_lo: 2; z = z_hi * 2 + z_lo), core: 2. Of those that a mesh axis runs over, the one named last changes fastest.
Arguments:
- tiles: bfloat16 [131072, 1536], P(('slide', 'seq')), may hold values from -6 to 6
- destination: int32 [131072], P(('slide', 'seq')), may hold values from 0 to 131071, as said below
- valid_len: int32 [8], replicated, may hold values from 4096 to 16384, as said below
- in_weight: bfloat16 [1536, 768], replicated, may hold values from -0.15625 to 0.15625
- norm_gain: float32 [768], replicated, may hold values from 0.25 to 1.75
- qkv_weight: bfloat16 [768, 2304], replicated, may hold values from -1 to 1
- out_weight: bfloat16 [768, 768], replicated, may hold values from -0.21875 to 0.21875
Outputs:
- encoded: bfloat16 [8, 16384, 768], P('slide', 'seq')
The draws below stay inside these ranges and needn't reach their ends.
Inputs may be any that keep to these rules, and one draw needn't show every extreme that they name: destination is a permutation of the 131072 flat positions; the rows of device d (devices in slide-major order) form consecutive blocks of 8 rows, block j holding only positions j * 1024 to (j + 1) * 1024 - 1. `valid_len`: one slide is full and one has exactly 4096 real tiles.
All inputs are finite; a program needn't handle non-finite values.
Results may differ from the reference program's by a relative error of at most 0.012.
Values may be sent and summed in bfloat16 or wider, within the bound.
A program may use at most 256 MiB of HBM per device.

```python
import jax
import jax.numpy as jnp
from jax import lax

E = 1536
D = 768
HEAD_COUNT = 12
HEAD_SIZE = 64
TILE_DEV = 1024
FIRST_SEGMENT = 8192
SECOND_SEGMENT = 32768
THIRD_SEGMENT = 65536
FIRST_DILATION = 4
SECOND_DILATION = 8
THIRD_DILATION = 16
SLIDES = 8
LEN = 16384
TOTAL = 131072
BLOCK = 8


def draw_destination(key, part):
    key = jax.random.fold_in(key, 11)
    count = TILE_DEV // BLOCK
    keys = jax.random.split(key, count)
    perms = jax.vmap(lambda single: jax.random.permutation(single, TILE_DEV))(keys)
    perms = perms.reshape(count, count, BLOCK)
    placed = perms + (jnp.arange(count, dtype=jnp.int32) * TILE_DEV)[:, None, None]
    return jnp.transpose(placed, (1, 0, 2)).reshape(-1).astype(jnp.int32)


def draw_valid_len(key, part):
    key = jax.random.fold_in(key, 12)
    first, second = jax.random.split(key)
    lengths = jax.random.randint(first, (SLIDES,), LEN // 4, LEN + 1)
    order = jax.random.permutation(second, SLIDES)
    lengths = lengths.at[order[0]].set(LEN).at[order[1]].set(LEN // 4)
    return lengths.astype(jnp.int32)


def draw_qkv_weight(key, part):
    key = jax.random.fold_in(key, 13)
    first = jax.random.fold_in(key, 0)
    base = jax.random.normal(first, (D, 3 * D), jnp.float32) * D ** (-0.5)
    return jnp.clip(base, -1.0, 1.0).astype(jnp.bfloat16)


def levels(key, extent, cuts, smallest, top_value):
    loudness = 1.0
    for axis_at, shards_of in cuts:
        steps = jax.random.uniform(jax.random.fold_in(jax.random.fold_in(key, 6), axis_at), (shards_of,), jnp.float32, smallest / len(cuts), top_value / len(cuts))
        loudness = loudness * jnp.repeat(jnp.exp(steps), extent[axis_at] // shards_of).reshape((-1,) + (1,) * (len(extent) - 1 - axis_at))
    return loudness


def centred(own_key, shape, deviation, reach, cuts=(), kind=jnp.bfloat16):
    values = jax.random.normal(own_key, shape, jnp.float32) * deviation
    if len(cuts) > 0:
        values = levels(own_key, shape, cuts, -0.22, 0.18) * values
    return jnp.clip(values, min=-reach, max=reach).astype(kind)


def setup_inputs(seed: int = 0) -> dict:
    splits = jax.random.split(jax.random.key(seed), 8)
    return {
        "tiles": centred(splits[0], (TOTAL, E), 1.0, 6.0, ((0, 128),)),
        "destination": draw_destination(jax.random.fold_in(splits[7], 71), 0),
        "valid_len": draw_valid_len(jax.random.fold_in(splits[7], 71), 0),
        "in_weight": centred(splits[3], (E, D), E ** -0.5, 0.15625),
        "norm_gain": jnp.clip(1.0 + 0.15 * jax.random.normal(splits[4], (D,), jnp.float32), 0.25, 1.75),
        "qkv_weight": draw_qkv_weight(jax.random.fold_in(splits[7], 71), 0),
        "out_weight": centred(splits[6], (D, D), D ** -0.5, 0.21875),
    }


def branch_summaries(query_tensor, key_tensor, value_tensor, valid_length, segment_length, dilation_rate):
    segment_span = min(segment_length, LEN)
    segment_total = LEN // segment_span
    row_total = segment_span // dilation_rate
    query_split5 = query_tensor.reshape(segment_total, row_total, dilation_rate, HEAD_COUNT, HEAD_SIZE)
    key_split5 = key_tensor.reshape(segment_total, row_total, dilation_rate, HEAD_COUNT, HEAD_SIZE)
    value_split5 = value_tensor.reshape(segment_total, row_total, dilation_rate, HEAD_COUNT, HEAD_SIZE)
    running_maximum = jnp.full((segment_total, row_total, dilation_rate, HEAD_COUNT), -1e+30, jnp.float32)
    denominator_full = jnp.zeros((segment_total, row_total, dilation_rate, HEAD_COUNT), jnp.float32)
    numerator_full = jnp.zeros((segment_total, row_total, dilation_rate, HEAD_COUNT, HEAD_SIZE), jnp.float32)
    scale = 1.0 / HEAD_SIZE ** 0.5
    for head_number in range(HEAD_COUNT):
        dilation_offset = head_number % dilation_rate
        qh = query_split5[:, :, dilation_offset, head_number].astype(jnp.float32)
        kh = key_split5[:, :, dilation_offset, head_number].astype(jnp.float32)
        vh = value_split5[:, :, dilation_offset, head_number].astype(jnp.float32)
        key_position = (jnp.arange(segment_total, dtype=jnp.int32)[:, None] * segment_span + jnp.arange(row_total, dtype=jnp.int32)[None, :] * dilation_rate + dilation_offset).astype(jnp.int32)
        scores = jnp.einsum('nqd,nkd->nqk', qh, kh) * scale
        scores = jnp.where((key_position < valid_length)[:, None, :], scores, -1e+30)
        top = lax.optimization_barrier(jnp.max(scores, axis=-1))
        expo = jnp.exp(scores - top[..., None])
        total = lax.optimization_barrier(jnp.sum(expo, axis=-1))
        numer = jnp.einsum('nqk,nkd->nqd', expo.astype(jnp.bfloat16).astype(jnp.float32), vh)
        running_maximum = running_maximum.at[:, :, dilation_offset, head_number].set(top)
        denominator_full = denominator_full.at[:, :, dilation_offset, head_number].set(total)
        numerator_full = numerator_full.at[:, :, dilation_offset, head_number].set(numer)
    return (running_maximum.reshape(LEN, HEAD_COUNT), denominator_full.reshape(LEN, HEAD_COUNT), numerator_full.reshape(LEN, HEAD_COUNT, HEAD_SIZE))

def one_slide(emb, valid_length, norm_gain, qkv_weight, out_weight):
    value_input = emb.astype(jnp.float32)
    mean = lax.optimization_barrier(jnp.mean(value_input, axis=-1, keepdims=True))
    var = lax.optimization_barrier(jnp.mean((value_input - mean) ** 2, axis=-1, keepdims=True))
    normed = ((value_input - mean) * lax.rsqrt(var + 1e-05) * norm_gain).astype(jnp.bfloat16)
    qkv = jnp.dot(normed, qkv_weight, preferred_element_type=jnp.float32).astype(jnp.bfloat16)
    query_tensor = qkv[:, :D]
    key_tensor = qkv[:, D:2 * D]
    value_tensor = qkv[:, 2 * D:]
    branch_result = [branch_summaries(query_tensor, key_tensor, value_tensor, valid_length, segment_length, dilation_rate) for segment_length, dilation_rate in ((FIRST_SEGMENT, FIRST_DILATION), (SECOND_SEGMENT, SECOND_DILATION), (THIRD_SEGMENT, THIRD_DILATION))]
    upper = jnp.maximum(jnp.maximum(branch_result[0][0], branch_result[1][0]), branch_result[2][0])
    denom = jnp.zeros((LEN, HEAD_COUNT), jnp.float32)
    numer = jnp.zeros((LEN, HEAD_COUNT, HEAD_SIZE), jnp.float32)
    for top, total, part in branch_result:
        factor = jnp.exp(top - upper)
        denom = denom + factor * total
        numer = numer + factor[..., None] * part
    query_position = jnp.arange(LEN, dtype=jnp.int32)
    covered_rows = (query_position[:, None] % FIRST_DILATION == jnp.arange(HEAD_COUNT, dtype=jnp.int32)[None, :] % FIRST_DILATION) & (query_position[:, None] < valid_length)
    safe = jnp.where(covered_rows, denom, 1.0)
    attn = jnp.where(covered_rows[..., None], numer / safe[..., None], 0.0).reshape(LEN, D).astype(jnp.bfloat16)
    return jnp.dot(attn, out_weight, preferred_element_type=jnp.float32).astype(jnp.bfloat16)

def reference(tiles, destination, valid_len, in_weight, norm_gain, qkv_weight, out_weight):
    proj = jnp.dot(tiles, in_weight, preferred_element_type=jnp.float32).astype(jnp.bfloat16)
    emb = jnp.zeros_like(proj).at[destination].set(proj).reshape(SLIDES, LEN, D)
    return lax.map(lambda item: one_slide(item[0], item[1], norm_gain, qkv_weight, out_weight), (emb, valid_len))
```

```python
import functools

import jax
import jax.numpy as jnp
from jax import lax
from jax.experimental import pallas as pl
from jax.experimental.pallas import tpu as pltpu
from jax.sharding import PartitionSpec as P

MESH = pl.DeviceIdType.MESH
SLIDES = 8
SEQ = 16
DEVICES = 128
ROWS = 1024
BLOCK = 8
E = 1536
D = 768
WIDE = 640
CHUNK = 256
BF = jnp.bfloat16
F32 = jnp.float32
I32 = jnp.int32


def iota(shape, dim):
    return lax.broadcasted_iota(I32, shape, dim)


def pick_columns(qkv, place):
    rows = qkv.shape[0]
    lane = iota((rows, 128), 1)
    cls = place & 3
    high = cls >= 2
    odd = (cls & 1) == 1
    low_lane = lane < 64

    def head(kind, group):
        at = kind * D + group * 256
        return jnp.where(high, qkv[:, at + 128 : at + 256], qkv[:, at : at + 128])

    def pair(left, right):
        moved = pltpu.roll(jnp.where(odd, left, right), 64, 1)
        return jnp.where(low_lane == odd, moved, jnp.where(odd, right, left))

    step = (place >> 2) & 3
    sorted_at = cls * 256 + (((step & 1) << 1) | (step >> 1)) * 64 + (place >> 4)
    ids = jnp.where(lane == 64, sorted_at >> 7, jnp.where(lane == 65, sorted_at & 127, 0)).astype(F32)
    q2 = head(0, 2) * 0.125
    q2 = jnp.where(odd, pltpu.roll(q2, 64, 1), q2)
    return (
        pair(head(0, 0) * 0.125, head(0, 1) * 0.125),
        jnp.where(low_lane, q2, ids),
        pair(head(1, 0), head(2, 0)),
        pair(head(1, 2), head(2, 2)),
        pair(head(1, 1), head(2, 1)),
    )


def project_kernel(tiles, dest, w_in, gain, w_qkv, recv, tiles_v, w_in_v, w_qkv_v, send, load_sem, send_sem, recv_sem, own_sem):
    slide = lax.axis_index("slide")
    seq = lax.axis_index("seq")
    me = slide * SEQ + seq
    chunks = ROWS // CHUNK
    per = CHUNK // BLOCK

    def chunk_at(step):
        return lax.rem(slide // 2 + step, chunks)

    loads = [pltpu.make_async_copy(w_in, w_in_v, load_sem.at[0]), pltpu.make_async_copy(w_qkv, w_qkv_v, load_sem.at[1])]
    for step in range(chunks):
        loads.append(
            pltpu.make_async_copy(
                tiles.at[pl.ds(pl.multiple_of(chunk_at(step) * CHUNK, CHUNK), CHUNK)],
                tiles_v.at[step],
                load_sem.at[2 + step],
            )
        )
    for index in (0, 2, 1, 3, 4, 5):
        loads[index].start()

    barrier = pltpu.get_barrier_semaphore()

    @pl.loop(1, DEVICES)
    def _(i):
        other = lax.rem(me + i, DEVICES)
        pl.semaphore_signal(barrier, inc=1, device_id=(other // SEQ, lax.rem(other, SEQ)), device_id_type=MESH)

    for step in range(chunks):
        chunk = chunk_at(step)
        if step == 0:
            loads[0].wait()
        loads[2 + step].wait()
        proj = jnp.dot(tiles_v[step], w_in_v[...], preferred_element_type=F32).astype(BF).astype(F32)
        mean = jnp.mean(proj, axis=-1, keepdims=True)
        centred = proj - mean
        var = jnp.mean(centred * centred, axis=-1, keepdims=True)
        normed = (centred * lax.rsqrt(var + 1e-05) * gain[...]).astype(BF)
        if step == 0:
            loads[1].wait()
        qkv = jnp.dot(normed, w_qkv_v[...], preferred_element_type=F32)
        eye = iota((128, 128), 0) == iota((128, 128), 1)
        places = []
        for part in range(CHUNK // 128):
            line = dest[pl.ds(chunk * (CHUNK // 128) + part, 1), :] & (ROWS - 1)
            places.append(jnp.sum(jnp.where(eye, line.astype(F32), 0.0), axis=1, keepdims=True))
        place = jnp.concatenate(places, axis=0).astype(I32)
        for index, block in enumerate(pick_columns(qkv, place)):
            send[pl.ds(chunk * per, per), :, index * 128 : (index + 1) * 128] = block.reshape(per, BLOCK, 128).astype(BF)
        if step == 0:
            pl.semaphore_wait(barrier, DEVICES - 1)

        @pl.loop(0, per)
        def _(i):
            other = chunk * per + lax.rem(seq * 2 + i, per)

            @pl.when(other != me)
            def _():
                pltpu.make_async_remote_copy(
                    src_ref=send.at[other],
                    dst_ref=recv.at[me],
                    send_sem=send_sem,
                    recv_sem=recv_sem,
                    device_id=(other // SEQ, lax.rem(other, SEQ)),
                    device_id_type=MESH,
                ).start()

    own = pltpu.make_async_copy(send.at[me], recv.at[me], own_sem)
    own.start()
    own.wait()
    rest = pl.ds(0, DEVICES - 1)
    pltpu.make_async_copy(send.at[rest], send.at[rest], send_sem).wait()
    pltpu.make_async_copy(recv.at[rest], recv.at[rest], recv_sem).wait()


def project(tiles, dest, w_in, gain, w_qkv):
    anywhere = pl.BlockSpec(memory_space=pl.ANY)
    vmem = pl.BlockSpec(memory_space=pltpu.VMEM)
    return pl.pallas_call(
        project_kernel,
        out_shape=jax.ShapeDtypeStruct((DEVICES, BLOCK, WIDE), BF),
        in_specs=[anywhere, vmem, anywhere, vmem, anywhere],
        out_specs=anywhere,
        scratch_shapes=[
            pltpu.VMEM((ROWS // CHUNK, CHUNK, E), BF),
            pltpu.VMEM((E, D), BF),
            pltpu.VMEM((D, 3 * D), BF),
            pltpu.VMEM((DEVICES, BLOCK, WIDE), BF),
            pltpu.SemaphoreType.DMA((2 + ROWS // CHUNK,)),
            pltpu.SemaphoreType.DMA,
            pltpu.SemaphoreType.DMA,
            pltpu.SemaphoreType.DMA,
        ],
        compiler_params=pltpu.CompilerParams(collective_id=0, has_side_effects=True, vmem_limit_bytes=48 * 1024 * 1024),
        name="project_send",
    )(tiles, dest, w_in, gain, w_qkv)


def attend_kernel(
    recv, valid, back, own, sib, x_own, x_sib, stage, q_op, k_op, v_op, result, attn,
    send_sem, recv_sem, sib_send, sib_recv, x_send, x_recv, xs_send, xs_recv, out_send, out_recv, own_sem,
):
    slide = lax.axis_index("slide")
    seq = lax.axis_index("seq")
    half = seq // 8
    row = lax.rem(seq // 4, 2)
    col = lax.rem(seq // 2, 2)
    core = lax.rem(seq, 2)

    def chip(d):
        return lax.rem(row + d // 2, 2), lax.rem(col + d % 2, 2)

    def slot(d):
        r, c = chip(d)
        return 2 * r + c

    def cls_of(d):
        r, c = chip(d)
        return 2 * lax.rem(r + half, 2) + c

    def device(d):
        return (slide, half * 8 + slot(d) * 2 + core)

    sibling = (slide, seq + 1 - 2 * core)
    cross = (slide, (1 - half) * 8 + (2 * (1 - row) + col) * 2 + core)
    partners = [device(1), device(2), device(3), sibling, cross]

    def cross_slot(d):
        return 2 * lax.rem(1 - row + d // 2, 2) + lax.rem(col + d % 2, 2)

    barrier = pltpu.get_barrier_semaphore()
    for other in partners:
        pl.semaphore_signal(barrier, inc=1, device_id=other, device_id_type=MESH)

    rows_in = recv[...]
    lane8 = iota((8, 128), 1)
    weigh = jnp.where(lane8 == 64, 128.0, jnp.where(lane8 == 65, 1.0, 0.0)).astype(BF)
    at = lax.dot_general(weigh, rows_in[:, 128:256], (((1,), (1,)), ((), ())), preferred_element_type=F32)
    at = at[0:1].astype(I32)

    def sort_class(cls):
        hit = (at - cls * 256) == iota((256, ROWS), 0)
        one_hot = jnp.where(hit, 1.0, 0.0).astype(BF)
        return jnp.dot(one_hot, rows_in, preferred_element_type=F32).astype(BF).reshape(4, 64, WIDE)

    def remote(src, dst, send, recv_, to):
        return pltpu.make_async_remote_copy(
            src_ref=src, dst_ref=dst, send_sem=send, recv_sem=recv_, device_id=to, device_id_type=MESH
        )

    mine = slot(0)
    sends = []
    first = {}
    for order, d in enumerate((3, 2, 1)):
        stage[d - 1] = sort_class(cls_of(d))
        if order == 0:
            pl.semaphore_wait(barrier, len(partners))
        first[d] = remote(stage.at[d - 1], own.at[:, mine], send_sem.at[d - 1], recv_sem.at[d - 1], device(d))
        first[d].start()
    own[:, pl.ds(mine, 1)] = sort_class(cls_of(0)).reshape(4, 1, 64, WIDE)

    sib_copies, x_copies, xs_copies = {}, {}, {}
    for d in (0, 2, 1, 3):
        if d > 0:
            first[d].wait_recv()
        s = slot(d)
        sib_copies[d] = remote(own.at[:, s, :, 256:WIDE], sib.at[:, s], sib_send.at[d], sib_recv.at[d], sibling)
        sib_copies[d].start()
        x_copies[d] = [
            remote(own.at[0:2, s, :, 256:512], x_own.at[:, s, :, 0:256], x_send.at[d, 0], x_recv.at[d, 0], cross),
            remote(own.at[2:4, s, :, 512:640], x_own.at[:, s, :, 256:384], x_send.at[d, 1], x_recv.at[d, 1], cross),
        ]
        for copy in x_copies[d]:
            copy.start()
    for d in range(4):
        sib_copies[d].wait_recv()

    cls = cls_of(0)
    length = valid[slide]
    lane = iota((256, 128), 1)
    low_lane = lane < 64
    key_row = iota((256, 128), 0)
    key_step = (key_row // 64) * 2048 + lax.rem(key_row, 64) * 16

    def keys(place, group, half_, core_, a, block):
        position = key_step + (half_ * 8192 + core_ * 1024 + cls + (a % 2) * 8 + (a // 2) * 4)
        bias = jnp.where((lane == 64) & (position >= length), -1e30, 0.0).astype(BF)
        k_op[group, place : place + 256, :] = jnp.where(low_lane, block, bias)
        v_op[group, place : place + 256, :] = jnp.where(low_lane, jnp.ones_like(block), block)

    tile_of = (2, 4, 3)
    order_of = ((0, 1, 2, 3), (2, 3, 0, 1), (1, 0, 2, 3))
    for group in range(3):
        at_lane = tile_of[group] * 128
        for index, a in enumerate(order_of[group]):
            keys(index * 512, group, half, core, a, own[a, :, :, at_lane : at_lane + 128].reshape(256, 128))
            keys(index * 512 + 256, group, half, 1 - core, a, sib[a, :, :, at_lane - 256 : at_lane - 128].reshape(256, 128))
            q = own[a, :, :, (group // 2) * 128 : (group // 2) * 128 + 128].reshape(256, 128).astype(F32)
            if group == 1:
                q = pltpu.roll(q, 64, 1)
            q_op[group, a] = jnp.where(low_lane, q, jnp.where(lane == 64, 1.0, 0.0)).astype(BF)

    contract = (((1,), (1,)), ((), ()))

    def finish(group, a, acc):
        out = acc / pltpu.roll(acc, 64, 1)
        position = key_step + (half * 8192 + core * 1024 + cls + lax.rem(a, 2) * 8 + (a // 2) * 4)
        result[group, a] = jnp.where(position < length, out, 0.0)

    @pl.loop(0, 6)
    def _(tile):
        group = tile // 2
        a = lax.rem(tile, 2) + 2 * (1 - lax.rem(group, 2))
        scores = lax.dot_general(q_op[group, a], k_op[group, 0:2048, :], contract, preferred_element_type=F32)
        top = jnp.max(scores, axis=1, keepdims=True)
        expo = jnp.exp(scores - top).astype(BF)
        finish(group, a, jnp.dot(expo, v_op[group, 0:2048, :], preferred_element_type=F32))

    for d in (0, 2, 1, 3):
        s = cross_slot(d)
        for copy in x_copies[d]:
            copy.wait_recv()
        xs_copies[d] = remote(x_own.at[:, s], x_sib.at[:, s], xs_send.at[d], xs_recv.at[d], sibling)
        xs_copies[d].start()
    for d in range(4):
        xs_copies[d].wait_recv()
    for group in range(3):
        at_lane = (tile_of[group] - 2) * 128
        for index in range(2):
            a = order_of[group][index]
            keys(2048 + index * 512, group, 1 - half, core, a, x_own[a % 2, :, :, at_lane : at_lane + 128].reshape(256, 128))
            keys(2304 + index * 512, group, 1 - half, 1 - core, a, x_sib[a % 2, :, :, at_lane : at_lane + 128].reshape(256, 128))

    @pl.loop(0, 6)
    def _(tile):
        group = tile // 2
        kind = lax.rem(tile, 2)
        a = 2 * lax.rem(group, 2) + lax.rem(kind + group // 2, 2)
        extra = (1 - kind).astype(F32)
        scores = lax.dot_general(q_op[group, a], k_op[group], contract, preferred_element_type=F32)
        top = jnp.max(scores, axis=1, keepdims=True)
        expo = jnp.exp(scores - top).astype(BF)
        acc = jnp.zeros((256, 128), F32)
        for begin, end, weight in (
            (0, 512, 2.0 + extra),
            (512, 1024, 2.0),
            (1024, 2048, 1.0),
            (2048, 2560, 1.0 + extra),
            (2560, 3072, 1.0),
        ):
            acc += weight * jnp.dot(expo[:, begin:end], v_op[group, begin:end, :], preferred_element_type=F32)
        finish(group, a, acc)

    for a in range(4):
        left = jnp.where(low_lane, pltpu.roll(result[0, a], 64, 1), result[1, a])
        right = jnp.where(low_lane, pltpu.roll(result[2, a], 64, 1), 0.0)
        attn[a, :, :, 0:128] = left.astype(BF).reshape(4, 64, 128)
        attn[a, :, :, 128:256] = right.astype(BF).reshape(4, 64, 128)
    outs = []
    for d in (3, 2, 1):
        copy = remote(attn.at[:, slot(d)], back.at[cls], out_send.at[d - 1], out_recv.at[d - 1], device(d))
        copy.start()
        outs.append(copy)
    own_copy = pltpu.make_async_copy(attn.at[:, mine], back.at[cls], own_sem)
    own_copy.start()
    own_copy.wait()
    for copy in outs:
        copy.wait()
    for d in range(4):
        if d > 0:
            first[d].wait_send()
        sib_copies[d].wait_send()
        for copy in x_copies[d]:
            copy.wait_send()
        xs_copies[d].wait_send()


def attend(recv, valid):
    vmem = pl.BlockSpec(memory_space=pltpu.VMEM)
    dma = pltpu.SemaphoreType.DMA
    return pl.pallas_call(
        attend_kernel,
        out_shape=jax.ShapeDtypeStruct((4, 4, 64, 256), BF),
        in_specs=[vmem, pl.BlockSpec(memory_space=pltpu.SMEM)],
        out_specs=pl.BlockSpec(memory_space=pl.ANY),
        scratch_shapes=[
            pltpu.VMEM((4, 4, 64, WIDE), BF),
            pltpu.VMEM((4, 4, 64, 384), BF),
            pltpu.VMEM((2, 4, 64, 384), BF),
            pltpu.VMEM((2, 4, 64, 384), BF),
            pltpu.VMEM((3, 4, 64, WIDE), BF),
            pltpu.VMEM((3, 4, 256, 128), BF),
            pltpu.VMEM((3, 3072, 128), BF),
            pltpu.VMEM((3, 3072, 128), BF),
            pltpu.VMEM((3, 4, 256, 128), F32),
            pltpu.VMEM((4, 4, 64, 256), BF),
            dma((3,)),
            dma((3,)),
            dma((4,)),
            dma((4,)),
            dma((4, 2)),
            dma((4, 2)),
            dma((4,)),
            dma((4,)),
            dma((3,)),
            dma((3,)),
            dma,
        ],
        compiler_params=pltpu.CompilerParams(collective_id=1, has_side_effects=True, vmem_limit_bytes=56 * 1024 * 1024),
        name="attend",
    )(recv, valid)


def output_kernel(rows_in, weight, out, mixed):
    @pl.when(pl.program_id(0) == 0)
    def _():
        for cls in range(4):
            parts = [weight[(cls + 4 * g) * 64 : (cls + 4 * g + 1) * 64, :] for g in range(3)]
            wide = jnp.concatenate(parts + [jnp.zeros((64, D), BF)], axis=0)
            block = jnp.dot(rows_in[cls * 256 : (cls + 1) * 256, :], wide, preferred_element_type=F32)
            mixed[cls * 256 : (cls + 1) * 256, :] = block.astype(BF)

    place = iota((256, ROWS), 0) + pl.program_id(0) * 256
    step = (place >> 2) & 3
    sorted_at = (place & 3) * 256 + (((step & 1) << 1) | (step >> 1)) * 64 + (place >> 4)
    one_hot = jnp.where(sorted_at == iota((256, ROWS), 1), 1.0, 0.0).astype(BF)
    out[...] = jnp.dot(one_hot, mixed[...], preferred_element_type=F32).astype(BF)


def output(rows_in, weight):
    return pl.pallas_call(
        output_kernel,
        grid=(4,),
        out_shape=jax.ShapeDtypeStruct((ROWS, D), BF),
        in_specs=[pl.BlockSpec((ROWS, 256), lambda i: (0, 0)), pl.BlockSpec((D, D), lambda i: (0, 0))],
        out_specs=pl.BlockSpec((256, D), lambda i: (i, 0)),
        scratch_shapes=[pltpu.VMEM((ROWS, D), BF)],
        compiler_params=pltpu.CompilerParams(vmem_limit_bytes=32 * 1024 * 1024),
        name="output",
    )(rows_in, weight)


def local(tiles, destination, valid_len, in_weight, norm_gain, qkv_weight, out_weight):
    recv = project(tiles, destination.reshape(8, 128), in_weight, norm_gain.reshape(1, D), qkv_weight)
    back = attend(recv.reshape(ROWS, WIDE), valid_len)
    return output(back.reshape(ROWS, 256), out_weight).reshape(1, ROWS, D)


def solution(mesh):
    in_specs = (P(("slide", "seq"), None), P(("slide", "seq")), P(), P(), P(), P(), P())
    return jax.shard_map(local, mesh=mesh, in_specs=in_specs, out_specs=P("slide", "seq", None), check_vma=False)
```

```python
import functools

import jax
import jax.numpy as jnp
from jax import lax
from jax.experimental import pallas as pl
from jax.experimental.pallas import tpu as pltpu
from jax.sharding import PartitionSpec as P

MESH = pl.DeviceIdType.MESH
SLIDES = 8
SEQ = 16
DEVICES = 128
ROWS = 1024
BLOCK = 8
E = 1536
D = 768
WIDE = 640
PLACES = 4
VMEM_LIMIT = 63 * 1024 * 1024
CHUNK = 256
BF = jnp.bfloat16
F32 = jnp.float32
I32 = jnp.int32


def iota(shape, dim):
    return lax.broadcasted_iota(I32, shape, dim)


def pick_columns(qkv, place):
    rows = qkv.shape[0]
    lane = iota((rows, 128), 1)
    cls = place & 3
    high = cls >= 2
    odd = (cls & 1) == 1
    low_lane = lane < 64

    def head(kind, group):
        at = kind * D + group * 256
        return jnp.where(high, qkv[:, at + 128 : at + 256], qkv[:, at : at + 128])

    def pair(left, right):
        moved = pltpu.roll(jnp.where(odd, left, right), 64, 1)
        return jnp.where(low_lane == odd, moved, jnp.where(odd, right, left))

    step = (place >> 2) & 3
    sorted_at = cls * 256 + (((step & 1) << 1) | (step >> 1)) * 64 + (place >> 4)
    ids = jnp.where(lane == 64, sorted_at >> 7, jnp.where(lane == 65, sorted_at & 127, 0)).astype(F32)
    q2 = head(0, 2) * 0.125
    q2 = jnp.where(odd, pltpu.roll(q2, 64, 1), q2)
    return (
        pair(head(0, 0) * 0.125, head(0, 1) * 0.125),
        jnp.where(low_lane, q2, ids),
        pair(head(1, 0), head(2, 0)),
        pair(head(1, 2), head(2, 2)),
        pair(head(1, 1), head(2, 1)),
    )


def project_kernel(tiles, dest, w_in, gain, w_qkv, recv, tiles_v, w_in_v, w_qkv_v, dest_v, gain_v, send, load_sem, send_sem, recv_sem, own_sem):
    slide = lax.axis_index("slide")
    seq = lax.axis_index("seq")
    me = slide * SEQ + seq
    across = seq // PLACES
    place_me = lax.rem(seq, PLACES)

    def place_at(step):
        return lax.rem(place_me + step, PLACES)

    loads = [
        pltpu.make_async_copy(w_in, w_in_v, load_sem.at[0]),
        pltpu.make_async_copy(w_qkv, w_qkv_v, load_sem.at[1]),
        pltpu.make_async_copy(dest, dest_v, load_sem.at[2]),
        pltpu.make_async_copy(gain, gain_v, load_sem.at[3]),
    ]
    for step in range(PLACES):
        loads.append(pltpu.make_async_copy(tiles.at[:, place_at(step)], tiles_v.at[step], load_sem.at[4 + step]))
    for index in (0, 4, 2, 3, 1, 5, 6, 7):
        loads[index].start()

    barrier = pltpu.get_barrier_semaphore()

    @pl.loop(1, DEVICES)
    def _(i):
        other = lax.rem(me + i, DEVICES)
        pl.semaphore_signal(barrier, inc=1, device_id=(other // SEQ, lax.rem(other, SEQ)), device_id_type=MESH)

    for step in range(PLACES):
        place = place_at(step)
        if step == 0:
            loads[0].wait()
        loads[4 + step].wait()
        x = tiles_v[step].reshape(CHUNK, E)
        proj = jnp.dot(x, w_in_v[...], preferred_element_type=F32).astype(BF).astype(F32)
        mean = jnp.mean(proj, axis=-1, keepdims=True)
        centred = proj - mean
        var = jnp.mean(centred * centred, axis=-1, keepdims=True)
        if step == 0:
            loads[3].wait()
        gains = jnp.concatenate([gain_v[i : i + 1, :] for i in range(D // 128)], axis=1)
        normed = (centred * lax.rsqrt(var + 1e-05) * gains).astype(BF)
        if step == 0:
            loads[1].wait()
        qkv = jnp.dot(normed, w_qkv_v[...], preferred_element_type=F32)
        if step == 0:
            loads[2].wait()
        lines = (dest_v[...] & (ROWS - 1)).astype(F32)
        lines = jnp.broadcast_to(lines.reshape(8, 1, 128), (8, 32, 128)).reshape(CHUNK, 128)
        r = iota((CHUNK, 128), 0)
        wanted = ((r >> 3) & 3) * 32 + place * 8 + (r & 7)
        position = jnp.sum(jnp.where(iota((CHUNK, 128), 1) == wanted, lines, 0.0), axis=1, keepdims=True).astype(I32)
        for index, block in enumerate(pick_columns(qkv, position)):
            send[:, place, :, index * 128 : (index + 1) * 128] = block.reshape(CHUNK // BLOCK, BLOCK, 128).astype(BF)
        if step == 0:
            pl.semaphore_wait(barrier, DEVICES - 1)

        @pl.loop(0, CHUNK // BLOCK)
        def _(i):
            to_slide = lax.rem(slide + i, SLIDES)
            to_across = lax.rem(across + i // SLIDES, 4)

            @pl.when((to_slide != slide) | (to_across != across) | (place != place_me))
            def _():
                pltpu.make_async_remote_copy(
                    src_ref=send.at[to_slide * 4 + to_across, place],
                    dst_ref=recv.at[me],
                    send_sem=send_sem,
                    recv_sem=recv_sem,
                    device_id=(to_slide, to_across * PLACES + place),
                    device_id_type=MESH,
                ).start()

    own = pltpu.make_async_copy(send.at[slide * 4 + across, place_me], recv.at[me], own_sem)
    own.start()
    own.wait()
    rest = pl.ds(0, DEVICES - 1)
    pltpu.make_async_copy(recv.at[rest], recv.at[rest], send_sem).wait()
    pltpu.make_async_copy(recv.at[rest], recv.at[rest], recv_sem).wait()


def project(tiles, dest, w_in, gain, w_qkv):
    hbm = pl.BlockSpec(memory_space=pltpu.HBM)
    return pl.pallas_call(
        project_kernel,
        out_shape=jax.ShapeDtypeStruct((DEVICES, BLOCK, WIDE), BF),
        in_specs=[hbm] * 5,
        out_specs=hbm,
        scratch_shapes=[
            pltpu.VMEM((PLACES, CHUNK // BLOCK, BLOCK, E), BF),
            pltpu.VMEM((E, D), BF),
            pltpu.VMEM((D, 3 * D), BF),
            pltpu.VMEM((8, 128), I32),
            pltpu.VMEM((D // 128, 128), F32),
            pltpu.VMEM((CHUNK // BLOCK, PLACES, BLOCK, WIDE), BF),
            pltpu.SemaphoreType.DMA((4 + PLACES,)),
            pltpu.SemaphoreType.DMA,
            pltpu.SemaphoreType.DMA,
            pltpu.SemaphoreType.DMA,
        ],
        compiler_params=pltpu.CompilerParams(collective_id=0, has_side_effects=True, vmem_limit_bytes=VMEM_LIMIT),
        name="project_send",
    )(tiles, dest, w_in, gain, w_qkv)


ARRIVAL = (0, 2, 1, 3)
TILE_OF = (2, 4, 3)
PAIR_OF = ((0, 1), (2, 3), (1, 0))
LN2 = (0.69140625, 0.0017409306)
LN3 = (1.1015625, -0.0029502113)


def key_table(rows, group, key_first, inner):
    lane = iota((rows, 128), 1)
    key = iota((rows, 128), 0) // 64 + key_first
    third, second = PAIR_OF[group]
    query = jnp.where(lane < 69, lane - 65, lane - 69)
    used = (lane >= 65) & (lane < 73)
    twice = used & ((query == third) | (query == second)) & ((key == third) | (key == second))
    thrice = used & (query == third) & (key == third)
    first = lane < 69
    ln2 = jnp.where(first, LN2[0], LN2[1])
    ln3 = jnp.where(first, LN3[0], LN3[1])
    if inner:
        return jnp.where(thrice, ln3, jnp.where(twice, ln2, 0.0))
    return jnp.where(thrice, ln2, 0.0)


def attend_kernel(
    recv, valid, back, own, sib, x_own, x_sib, stage, q_op, k_op, v_op, xk_op, xv_op, tops, sums, attn, q_tab, k_tab, x_tab,
    send_sem, recv_sem, sib_send, sib_recv, x_send, x_recv, xs_send, xs_recv, out_send, out_recv, own_sem,
):
    slide = lax.axis_index("slide")
    seq = lax.axis_index("seq")
    half = seq // 8
    row = lax.rem(seq // 4, 2)
    col = lax.rem(seq // 2, 2)
    core = lax.rem(seq, 2)

    def slot(d):
        return 2 * lax.rem(row + d // 2, 2) + lax.rem(col + d % 2, 2)

    def cross_slot(d):
        return 2 * lax.rem(1 - row + d // 2, 2) + lax.rem(col + d % 2, 2)

    def cls_of(d):
        return 2 * lax.rem(row + d // 2 + half, 2) + lax.rem(col + d % 2, 2)

    def device(d):
        return (slide, half * 8 + slot(d) * 2 + core)

    sibling = (slide, seq + 1 - 2 * core)
    cross = (slide, (1 - half) * 8 + cross_slot(0) * 2 + core)
    partners = [device(1), device(2), device(3), sibling, cross]

    barrier = pltpu.get_barrier_semaphore()
    for other in partners:
        pl.semaphore_signal(barrier, inc=1, device_id=other, device_id_type=MESH)

    rows_in = recv[...]
    lane8 = iota((8, 128), 1)
    weigh = jnp.where(lane8 == 64, 128.0, jnp.where(lane8 == 65, 1.0, 0.0)).astype(BF)
    at = lax.dot_general(weigh, rows_in[:, 128:256], (((1,), (1,)), ((), ())), preferred_element_type=F32)
    at = at[0:1].astype(I32)

    def sort_class(cls):
        hit = (at - cls * 256) == iota((256, ROWS), 0)
        one_hot = jnp.where(hit, 1.0, 0.0).astype(BF)
        return jnp.dot(one_hot, rows_in, preferred_element_type=F32).astype(BF).reshape(4, 64, WIDE)

    def remote(src, dst, send, recv_, to):
        return pltpu.make_async_remote_copy(
            src_ref=src, dst_ref=dst, send_sem=send, recv_sem=recv_, device_id=to, device_id_type=MESH
        )

    first = {}
    for order, d in enumerate(ARRIVAL[1:]):
        stage[d - 1] = sort_class(cls_of(d))
        if order == 0:
            pl.semaphore_wait(barrier, len(partners))
        first[d] = remote(stage.at[d - 1], own.at[d], send_sem.at[d - 1], recv_sem.at[d - 1], device(d))
        first[d].start()
    own[0] = sort_class(cls_of(0))

    sib_copies, x_copies, xs_copies = {}, {}, {}

    def arrive(d):
        if d > 0:
            first[d].wait_recv()
        sib_copies[d] = remote(own.at[d, :, :, 256:WIDE], sib.at[d], sib_send.at[d], sib_recv.at[d], sibling)
        sib_copies[d].start()
        x_copies[d] = [
            remote(own.at[d, 0:2, :, 256:512], x_own.at[d, :, :, 0:256], x_send.at[d, 0], x_recv.at[d, 0], cross),
            remote(own.at[d, 2:4, :, 512:640], x_own.at[d, :, :, 256:384], x_send.at[d, 1], x_recv.at[d, 1], cross),
        ]
        for copy in x_copies[d]:
            copy.start()

    def arrive_cross(d):
        for copy in x_copies[d]:
            copy.wait_recv()
        xs_copies[d] = remote(x_own.at[d], x_sib.at[d], xs_send.at[d], xs_recv.at[d], sibling)
        xs_copies[d].start()

    cls = cls_of(0)
    length = valid[slide]
    lane = iota((256, 128), 1)
    low_lane = lane < 64
    line = iota((256, 128), 0)
    residue = line // 64
    steps = lax.rem(line, 64) * 16 + lax.rem(residue, 2) * 8 + (residue // 2) * 4

    def start_of(half_, slot_, core_):
        return half_ * 8192 + slot_ * 2048 + core_ * 1024 + cls

    q_tab[...] = jnp.where((lane == 64) | (lane == 65 + residue) | (lane == 69 + residue), 1.0, 0.0).astype(BF)
    for group in range(3):
        k_tab[group] = key_table(256, group, 0, True).astype(BF)
        x_tab[group] = key_table(128, group, 2 * (group % 2), False).astype(BF)

    def prepare(e):
        d = ARRIVAL[e]
        sib_copies[d].wait_recv()
        for source, core_ in ((own, core), (sib, 1 - core)):
            masked = (lane == 64) & (steps + start_of(half, slot(d), core_) >= length)
            at_row = e * 512 + (0 if source is own else 256)
            for group in range(3):
                at_lane = TILE_OF[group] * 128 - (0 if source is own else 256)
                block = source[d, :, :, at_lane : at_lane + 128].reshape(256, 128)
                bias = jnp.where(masked, jnp.full_like(block, -1e30), k_tab[group])
                k_op[group, at_row : at_row + 256, :] = jnp.where(low_lane, block, bias)
                v_op[group, at_row : at_row + 256, :] = jnp.where(low_lane, jnp.ones_like(block), block)
        for group in range(3):
            at_lane = (group // 2) * 128
            q = own[d, :, :, at_lane : at_lane + 128].reshape(256, 128)
            if group == 1:
                q = pltpu.roll(q.astype(F32), 64, 1).astype(BF)
            q_op[group, e] = jnp.where(low_lane, q, q_tab[...])

    def prepare_cross(e):
        d = ARRIVAL[e]
        xs_copies[d].wait_recv()
        for source, core_ in ((x_own, core), (x_sib, 1 - core)):
            at_row = e * 256 + (0 if source is x_own else 128)
            for group in range(3):
                at_lane = TILE_OF[group] * 128 - 256
                block = source[d, :, :, at_lane : at_lane + 128].reshape(128, 128)
                position = steps[0:128] + start_of(1 - half, cross_slot(d), core_) + 4 * (group % 2)
                masked = (lane[0:128] == 64) & (position >= length)
                bias = jnp.where(masked, jnp.full_like(block, -1e30), x_tab[group])
                xk_op[group, at_row : at_row + 128, :] = jnp.where(low_lane[0:128], block, bias)
                xv_op[group, at_row : at_row + 128, :] = jnp.where(low_lane[0:128], jnp.ones_like(block), block)

    contract = (((1,), (1,)), ((), ()))

    def wide(column, count):
        return jnp.concatenate([column] * count, axis=1)

    def mix(q, keys, values, state):
        scores = lax.dot_general(q, keys, contract, preferred_element_type=F32)
        top = jnp.broadcast_to(jnp.max(scores, axis=1, keepdims=True), (q.shape[0], 128))
        if state is not None:
            top = jnp.maximum(state[0], top)
        expo = jnp.exp(scores - wide(top, scores.shape[1] // 128)).astype(BF)
        acc = jnp.dot(expo, values, preferred_element_type=F32)
        if state is not None:
            acc += state[1] * jnp.exp(state[0] - top)
        return top, acc

    def parts(group, todo):
        states = [None if fresh else (tops[group, e], sums[group, e]) for e, _, _, fresh in todo]
        found = [
            mix(q_op[group, e], k_op[group, begin:end, :], v_op[group, begin:end, :], state)
            for (e, begin, end, _), state in zip(todo, states)
        ]
        for (e, _, _, _), (top, acc) in zip(todo, found):
            tops[group, e] = top
            sums[group, e] = acc

    def cross_parts(groups, begin, end):
        todo = []
        for group in groups:
            rows = pl.ds(pl.multiple_of(128 * lax.rem(group, 2), 128), 128)
            for both in ((0, 1), (2, 3)):
                todo.append((group, rows, both))

        def load(ref, group, rows, both):
            return jnp.concatenate([ref[group, e, rows, :] for e in both], axis=0)

        states = [(load(tops, *what), load(sums, *what)) for what in todo]
        queries = [load(q_op, *what) for what in todo]
        found = [
            mix(q, xk_op[what[0], begin:end, :], xv_op[what[0], begin:end, :], state)
            for what, q, state in zip(todo, queries, states)
        ]
        for (group, rows, both), (top, acc) in zip(todo, found):
            for index, e in enumerate(both):
                tops[group, e, rows, :] = top[index * 128 : index * 128 + 128]
                sums[group, e, rows, :] = acc[index * 128 : index * 128 + 128]

    arrive(0)
    prepare(0)
    for group in range(3):
        parts(group, [(0, 0, 512, True)])
    arrive(2)
    arrive(1)
    prepare(1)
    prepare(2)

    @pl.loop(0, 3)
    def _(group):
        parts(group, [(0, 512, 1536, False), (1, 0, 1536, True), (2, 0, 1536, True)])

    arrive(3)
    for d in (0, 2, 1):
        arrive_cross(d)
    prepare(3)

    @pl.loop(0, 3)
    def _(group):
        parts(group, [(3, 0, 2048, True)] + [(e, 1536, 2048, False) for e in range(3)])

    def finish(group, e, begin):
        acc = sums[group, e, begin : begin + 128, :]
        position = steps[begin : begin + 128] + start_of(half, slot(ARRIVAL[e]), core)
        return jnp.where(position < length, acc / pltpu.roll(acc, 64, 1), 0.0)

    outs = []

    def give(turn):
        wide, narrow = (128, 0) if turn == 0 else (0, 128)
        for e in (3, 1, 2, 0):
            d = ARRIVAL[e]
            low, high = finish(0, e, wide), finish(2, e, wide)
            middle = finish(1, e, narrow)
            joined = jnp.where(low_lane[0:128], pltpu.roll(low, 64, 1), high)
            packed = jnp.where(low_lane[0:64], pltpu.roll(middle[0:64], 64, 1), middle[64:128])
            attn[d, 3 * turn : 3 * turn + 2] = joined.astype(BF).reshape(2, 64, 128)
            attn[d, 3 * turn + 2] = packed.astype(BF)
            src, dst = attn.at[d, pl.ds(3 * turn, 3)], back.at[cls, pl.ds(3 * turn, 3)]
            if d > 0:
                copy = remote(src, dst, out_send.at[turn, d - 1], out_recv.at[turn, d - 1], device(d))
            else:
                copy = pltpu.make_async_copy(src, dst, own_sem.at[turn])
            copy.start()
            outs.append(copy)

    give(0)
    arrive_cross(3)
    for e in range(3):
        prepare_cross(e)

    @pl.loop(0, 3)
    def _(group):
        cross_parts([group], 0, 768)

    prepare_cross(3)
    cross_parts(range(3), 768, 1024)
    give(1)
    for copy in outs:
        copy.wait()
    for d in range(4):
        if d > 0:
            first[d].wait_send()
        sib_copies[d].wait_send()
        for copy in x_copies[d]:
            copy.wait_send()
        xs_copies[d].wait_send()


def attend(recv, valid):
    vmem = pl.BlockSpec(memory_space=pltpu.VMEM)
    dma = pltpu.SemaphoreType.DMA
    return pl.pallas_call(
        attend_kernel,
        out_shape=jax.ShapeDtypeStruct((4, 6, 64, 128), BF),
        in_specs=[vmem, pl.BlockSpec(memory_space=pltpu.SMEM)],
        out_specs=pl.BlockSpec(memory_space=pltpu.HBM),
        scratch_shapes=[
            pltpu.VMEM((4, 4, 64, WIDE), BF),
            pltpu.VMEM((4, 4, 64, 384), BF),
            pltpu.VMEM((4, 2, 64, 384), BF),
            pltpu.VMEM((4, 2, 64, 384), BF),
            pltpu.VMEM((3, 4, 64, WIDE), BF),
            pltpu.VMEM((3, 4, 256, 128), BF),
            pltpu.VMEM((3, 2048, 128), BF),
            pltpu.VMEM((3, 2048, 128), BF),
            pltpu.VMEM((3, 1024, 128), BF),
            pltpu.VMEM((3, 1024, 128), BF),
            pltpu.VMEM((3, 4, 256, 128), F32),
            pltpu.VMEM((3, 4, 256, 128), F32),
            pltpu.VMEM((4, 6, 64, 128), BF),
            pltpu.VMEM((256, 128), BF),
            pltpu.VMEM((3, 256, 128), BF),
            pltpu.VMEM((3, 128, 128), BF),
            dma((3,)),
            dma((3,)),
            dma((4,)),
            dma((4,)),
            dma((4, 2)),
            dma((4, 2)),
            dma((4,)),
            dma((4,)),
            dma((2, 3)),
            dma((2, 3)),
            dma((2,)),
        ],
        compiler_params=pltpu.CompilerParams(collective_id=1, has_side_effects=True, vmem_limit_bytes=VMEM_LIMIT),
        name="attend",
    )(recv, valid)


def output_kernel(rows_in, weight, out, mixed):
    @pl.when(pl.program_id(0) == 0)
    def _():
        for cls in range(4):
            w0, w1, w2 = [weight[(cls + 4 * g) * 64 : (cls + 4 * g + 1) * 64, :] for g in range(3)]
            zero = jnp.zeros((64, D), BF)
            w02 = jnp.concatenate([w0, w2], axis=0)
            ends = (jnp.concatenate([w1, zero], axis=0), jnp.concatenate([zero, w1], axis=0))
            rows = jnp.concatenate([rows_in[cls, i] for i in (3, 4, 0, 1)], axis=0)
            block = jnp.dot(rows, w02, preferred_element_type=F32)
            for a in range(4):
                middle = rows_in[cls, 2 if a < 2 else 5]
                total = block[a * 64 : a * 64 + 64] + jnp.dot(middle, ends[a % 2], preferred_element_type=F32)
                mixed[cls * 256 + a * 64 : cls * 256 + a * 64 + 64, :] = total.astype(BF)

    place = iota((256, ROWS), 0) + pl.program_id(0) * 256
    step = (place >> 2) & 3
    sorted_at = (place & 3) * 256 + (((step & 1) << 1) | (step >> 1)) * 64 + (place >> 4)
    one_hot = jnp.where(sorted_at == iota((256, ROWS), 1), 1.0, 0.0).astype(BF)
    out[...] = jnp.dot(one_hot, mixed[...], preferred_element_type=F32).astype(BF)


def output(rows_in, weight):
    return pl.pallas_call(
        output_kernel,
        grid=(4,),
        out_shape=jax.ShapeDtypeStruct((ROWS, D), BF),
        in_specs=[pl.BlockSpec((4, 6, 64, 128), lambda i: (0, 0, 0, 0)), pl.BlockSpec((D, D), lambda i: (0, 0))],
        out_specs=pl.BlockSpec((256, D), lambda i: (i, 0)),
        scratch_shapes=[pltpu.VMEM((ROWS, D), BF)],
        compiler_params=pltpu.CompilerParams(vmem_limit_bytes=32 * 1024 * 1024),
        name="output",
    )(rows_in, weight)


def local(tiles, destination, valid_len, in_weight, norm_gain, qkv_weight, out_weight):
    recv = project(tiles.reshape(CHUNK // BLOCK, PLACES, BLOCK, E), destination.reshape(8, 128), in_weight, norm_gain.reshape(D // 128, 128), qkv_weight)
    back = attend(recv.reshape(ROWS, WIDE), valid_len)
    return output(back, out_weight).reshape(1, ROWS, D)


def solution(mesh):
    in_specs = (P(("slide", "seq"), None), P(("slide", "seq")), P(), P(), P(), P(), P())
    return jax.shard_map(local, mesh=mesh, in_specs=in_specs, out_specs=P("slide", "seq", None), check_vma=False)
```

```python
import functools

import jax
import jax.numpy as jnp
from jax import lax
from jax.experimental import pallas as pl
from jax.experimental.pallas import tpu as pltpu
from jax.sharding import PartitionSpec as P

MESH = pl.DeviceIdType.MESH
SLIDES = 8
SEQ = 16
DEVICES = 128
ROWS = 1024
BLOCK = 8
E = 1536
D = 768
WIDE = 640
PLACES = 4
VMEM_LIMIT = 63 * 1024 * 1024
CHUNK = 256
BF = jnp.bfloat16
F32 = jnp.float32
I32 = jnp.int32


def iota(shape, dim):
    return lax.broadcasted_iota(I32, shape, dim)


def pick_columns(qkv, place):
    rows = qkv.shape[0]
    lane = iota((rows, 128), 1)
    cls = place & 3
    high = cls >= 2
    odd = (cls & 1) == 1
    low_lane = lane < 64

    def head(kind, group):
        at = kind * D + group * 256
        return jnp.where(high, qkv[:, at + 128 : at + 256], qkv[:, at : at + 128])

    def pair(left, right):
        moved = pltpu.roll(jnp.where(odd, left, right), 64, 1)
        return jnp.where(low_lane == odd, moved, jnp.where(odd, right, left))

    step = (place >> 2) & 3
    sorted_at = cls * 256 + (((step & 1) << 1) | (step >> 1)) * 64 + (place >> 4)
    ids = jnp.where(lane == 64, sorted_at >> 7, jnp.where(lane == 65, sorted_at & 127, 0)).astype(F32)
    q2 = head(0, 2) * 0.125
    q2 = jnp.where(odd, pltpu.roll(q2, 64, 1), q2)
    return (
        pair(head(0, 0) * 0.125, head(0, 1) * 0.125),
        jnp.where(low_lane, q2, ids),
        pair(head(1, 0), head(2, 0)),
        pair(head(1, 2), head(2, 2)),
        pair(head(1, 1), head(2, 1)),
    )


def project_kernel(tiles, dest, w_in, gain, w_qkv, recv, tiles_v, w_in_v, w_qkv_v, dest_v, gain_v, send, load_sem, send_sem, recv_sem, own_sem):
    slide = lax.axis_index("slide")
    seq = lax.axis_index("seq")
    me = slide * SEQ + seq
    across = seq // PLACES
    place_me = lax.rem(seq, PLACES)

    def place_at(step):
        return lax.rem(place_me + step, PLACES)

    loads = [
        pltpu.make_async_copy(w_in, w_in_v, load_sem.at[0]),
        pltpu.make_async_copy(w_qkv, w_qkv_v, load_sem.at[1]),
        pltpu.make_async_copy(dest, dest_v, load_sem.at[2]),
        pltpu.make_async_copy(gain, gain_v, load_sem.at[3]),
    ]
    for step in range(PLACES):
        loads.append(pltpu.make_async_copy(tiles.at[:, place_at(step)], tiles_v.at[step], load_sem.at[4 + step]))
    for index in (0, 4, 2, 3, 1, 5, 6, 7):
        loads[index].start()

    barrier = pltpu.get_barrier_semaphore()

    @pl.loop(1, DEVICES)
    def _(i):
        other = lax.rem(me + i, DEVICES)
        pl.semaphore_signal(barrier, inc=1, device_id=(other // SEQ, lax.rem(other, SEQ)), device_id_type=MESH)

    for step in range(PLACES):
        place = place_at(step)
        if step == 0:
            loads[0].wait()
        loads[4 + step].wait()
        x = tiles_v[step].reshape(CHUNK, E)
        proj = jnp.dot(x, w_in_v[...], preferred_element_type=F32).astype(BF).astype(F32)
        mean = jnp.mean(proj, axis=-1, keepdims=True)
        centred = proj - mean
        var = jnp.mean(centred * centred, axis=-1, keepdims=True)
        if step == 0:
            loads[3].wait()
        gains = jnp.concatenate([gain_v[i : i + 1, :] for i in range(D // 128)], axis=1)
        normed = (centred * lax.rsqrt(var + 1e-05) * gains).astype(BF)
        if step == 0:
            loads[1].wait()
        qkv = jnp.dot(normed, w_qkv_v[...], preferred_element_type=F32)
        if step == 0:
            loads[2].wait()
        lines = (dest_v[...] & (ROWS - 1)).astype(F32)
        lines = jnp.broadcast_to(lines.reshape(8, 1, 128), (8, 32, 128)).reshape(CHUNK, 128)
        r = iota((CHUNK, 128), 0)
        wanted = ((r >> 3) & 3) * 32 + place * 8 + (r & 7)
        position = jnp.sum(jnp.where(iota((CHUNK, 128), 1) == wanted, lines, 0.0), axis=1, keepdims=True).astype(I32)
        for index, block in enumerate(pick_columns(qkv, position)):
            send[:, place, :, index * 128 : (index + 1) * 128] = block.reshape(CHUNK // BLOCK, BLOCK, 128).astype(BF)
        if step == 0:
            pl.semaphore_wait(barrier, DEVICES - 1)

        @pl.loop(0, CHUNK // BLOCK)
        def _(i):
            to_slide = lax.rem(slide + i, SLIDES)
            to_across = lax.rem(across + i // SLIDES, 4)

            @pl.when((to_slide != slide) | (to_across != across) | (place != place_me))
            def _():
                pltpu.make_async_remote_copy(
                    src_ref=send.at[to_slide * 4 + to_across, place],
                    dst_ref=recv.at[me],
                    send_sem=send_sem,
                    recv_sem=recv_sem,
                    device_id=(to_slide, to_across * PLACES + place),
                    device_id_type=MESH,
                ).start()

    own = pltpu.make_async_copy(send.at[slide * 4 + across, place_me], recv.at[me], own_sem)
    own.start()
    own.wait()
    rest = pl.ds(0, DEVICES - 1)
    pltpu.make_async_copy(recv.at[rest], recv.at[rest], send_sem).wait()
    pltpu.make_async_copy(recv.at[rest], recv.at[rest], recv_sem).wait()


def project(tiles, dest, w_in, gain, w_qkv):
    hbm = pl.BlockSpec(memory_space=pltpu.HBM)
    return pl.pallas_call(
        project_kernel,
        out_shape=jax.ShapeDtypeStruct((DEVICES, BLOCK, WIDE), BF),
        in_specs=[hbm] * 5,
        out_specs=hbm,
        scratch_shapes=[
            pltpu.VMEM((PLACES, CHUNK // BLOCK, BLOCK, E), BF),
            pltpu.VMEM((E, D), BF),
            pltpu.VMEM((D, 3 * D), BF),
            pltpu.VMEM((8, 128), I32),
            pltpu.VMEM((D // 128, 128), F32),
            pltpu.VMEM((CHUNK // BLOCK, PLACES, BLOCK, WIDE), BF),
            pltpu.SemaphoreType.DMA((4 + PLACES,)),
            pltpu.SemaphoreType.DMA,
            pltpu.SemaphoreType.DMA,
            pltpu.SemaphoreType.DMA,
        ],
        compiler_params=pltpu.CompilerParams(collective_id=0, has_side_effects=True, vmem_limit_bytes=VMEM_LIMIT),
        name="project_send",
    )(tiles, dest, w_in, gain, w_qkv)


ARRIVAL = (0, 2, 1, 3)
PAIR_OF = ((0, 1), (2, 3), (1, 0))
LN2 = (0.69140625, 0.0017409306)
LN3 = (1.1015625, -0.0029502113)
PAIRS = (0, 4, 2)


def key_table(group, inner):
    lane = iota((128, 128), 1)
    key = iota((128, 128), 0) // 64 + 2 * (group % 2)
    third, second = PAIR_OF[group]
    query = jnp.where(lane < 69, lane - 65, lane - 69)
    used = (lane >= 65) & (lane < 73)
    twice = used & ((query == third) | (query == second))
    thrice = used & (query == third) & (key == third)
    first = lane < 69
    ln2 = jnp.where(first, LN2[0], LN2[1])
    ln3 = jnp.where(first, LN3[0], LN3[1])
    if inner:
        return jnp.where(thrice, ln3, jnp.where(twice, ln2, 0.0))
    return jnp.where(thrice, ln2, 0.0)


def attend_kernel(
    recv, valid, back, own, sib, x_own, x_sib, stage, q_op, k_op, v_op, xk_op, xv_op, tops, sums, attn, q_tab, k_tab, x_tab,
    send_sem, recv_sem, sib_send, sib_recv, x_send, x_recv, xs_send, xs_recv, out_send, out_recv, own_sem,
):
    slide = lax.axis_index("slide")
    seq = lax.axis_index("seq")
    half = seq // 8
    row = lax.rem(seq // 4, 2)
    col = lax.rem(seq // 2, 2)
    core = lax.rem(seq, 2)

    def slot(d):
        return 2 * lax.rem(row + d // 2, 2) + lax.rem(col + d % 2, 2)

    def cross_slot(d):
        return 2 * lax.rem(1 - row + d // 2, 2) + lax.rem(col + d % 2, 2)

    def cls_of(d):
        return 2 * lax.rem(row + d // 2 + half, 2) + lax.rem(col + d % 2, 2)

    def device(d):
        return (slide, half * 8 + slot(d) * 2 + core)

    sibling = (slide, seq + 1 - 2 * core)
    cross = (slide, (1 - half) * 8 + cross_slot(0) * 2 + core)
    partners = [device(1), device(2), device(3), sibling, cross]

    barrier = pltpu.get_barrier_semaphore()
    for other in partners:
        pl.semaphore_signal(barrier, inc=1, device_id=other, device_id_type=MESH)

    rows_in = recv[...]
    lane8 = iota((8, 128), 1)
    weigh = jnp.where(lane8 == 64, 128.0, jnp.where(lane8 == 65, 1.0, 0.0)).astype(BF)
    at = lax.dot_general(weigh, rows_in[:, 128:256], (((1,), (1,)), ((), ())), preferred_element_type=F32)
    at = at[0:1].astype(I32)
    low64 = iota((64, 128), 1) < 64

    def sort_class(cls, ref):
        hit = (at - cls * 256) == iota((256, ROWS), 0)
        one_hot = jnp.where(hit, 1.0, 0.0).astype(BF)
        found = jnp.dot(one_hot, rows_in, preferred_element_type=F32)

        def tile(a, t):
            return found[a * 64 : a * 64 + 64, t * 128 : t * 128 + 128]

        for index, (t, a) in enumerate(((2, 0), (3, 0), (4, 2))):
            for i in range(2):
                ref[2 * index + i] = tile(a + i, t).astype(BF)
                ref[12 + 2 * index + i] = tile((a + 2) % 4 + i, t).astype(BF)
        for a in range(4):
            ref[6 + a] = tile(a, 0).astype(BF)
        for i in range(2):
            ref[10 + i] = jnp.where(low64, tile(2 * i, 1), pltpu.roll(tile(2 * i + 1, 1), 64, 1)).astype(BF)

    def remote(src, dst, send, recv_, to):
        return pltpu.make_async_remote_copy(
            src_ref=src, dst_ref=dst, send_sem=send, recv_sem=recv_, device_id=to, device_id_type=MESH
        )

    third = {}

    def send(d, turn):
        part = pl.ds(6 * turn, 6)
        copy = remote(
            stage.at[d - 1, part], own.at[d, part], send_sem.at[d - 1, turn], recv_sem.at[d - 1, turn], device(d)
        )
        copy.start()
        third[d, turn] = copy

    for order, d in enumerate(ARRIVAL[1:]):
        sort_class(cls_of(d), stage.at[d - 1])
        if order == 0:
            pl.semaphore_wait(barrier, len(partners))
        send(d, 0)
    sort_class(cls_of(0), own.at[0])

    sib_copies, x_copies, xs_copies = {}, {}, {}

    def share(d, turn):
        if d > 0:
            third[d, turn].wait_recv()
        to = 0 if turn == 0 else 6
        copy = remote(
            own.at[d, pl.ds(6 * turn, 6)], sib.at[d, pl.ds(to, 6)], sib_send.at[d, to // 6], sib_recv.at[d, to // 6], sibling
        )
        copy.start()
        sib_copies[d, turn] = copy
        if turn == 0:
            x_copies[d] = remote(own.at[d, pl.ds(0, 6)], x_own.at[d], x_send.at[d], x_recv.at[d], cross)
            x_copies[d].start()

    def share_cross(d):
        x_copies[d].wait_recv()
        xs_copies[d] = remote(x_own.at[d], x_sib.at[d], xs_send.at[d], xs_recv.at[d], sibling)
        xs_copies[d].start()

    cls = cls_of(0)
    length = valid[slide]
    lane = iota((128, 128), 1)
    low_lane = lane < 64
    line = iota((128, 128), 0)
    steps = lax.rem(line, 64) * 16 + (line // 64) * 8

    def start_of(half_, slot_, core_):
        return half_ * 8192 + slot_ * 2048 + core_ * 1024 + cls

    for pair in range(2):
        residue = line // 64 + 2 * pair
        ones = jnp.where((lane == 64) | (lane == 65 + residue) | (lane == 69 + residue), 1.0, 0.0)
        q_tab[pair] = ones.astype(BF)
    for group in range(3):
        k_tab[group] = key_table(group, True).astype(BF)
        x_tab[group] = key_table(group, False).astype(BF)

    def keys(k_ref, v_ref, group, at_row, block, position, table):
        block = block.reshape(128, 128)
        bias = jnp.where((lane == 64) & (position >= length), jnp.full_like(block, -1e30), table)
        k_ref[group, at_row : at_row + 128, :] = jnp.where(low_lane, block, bias)
        v_ref[group, at_row : at_row + 128, :] = jnp.where(low_lane, jnp.ones_like(block), block)

    def prepare_keys(e, turn):
        d = ARRIVAL[e]
        sib_copies[d, turn].wait_recv()
        for source, core_ in ((own, core), (sib, 1 - core)):
            mine = source is own
            for group in range(3):
                at_tile = PAIRS[group] + (0 if turn == 0 else 12 if mine else 6)
                at_row = (0 if turn == 0 else 1024) + e * 256 + (0 if mine else 128)
                offset = 4 * (group % 2 if turn == 0 else 1 - group % 2)
                position = steps + (start_of(half, slot(d), core_) + offset)
                table = k_tab[group] if turn == 0 else jnp.zeros((128, 128), BF)
                keys(k_op, v_op, group, at_row, source[d, at_tile : at_tile + 2], position, table)

    def prepare_cross(e):
        d = ARRIVAL[e]
        xs_copies[d].wait_recv()
        for source, core_ in ((x_own, core), (x_sib, 1 - core)):
            for group in range(3):
                at_row = e * 256 + (0 if source is x_own else 128)
                position = steps + (start_of(1 - half, cross_slot(d), core_) + 4 * (group % 2))
                block = source[d, PAIRS[group] : PAIRS[group] + 2]
                keys(xk_op, xv_op, group, at_row, block, position, x_tab[group])

    def prepare_queries(e):
        d = ARRIVAL[e]
        for pair in range(2):
            both = own[d, 6 + 2 * pair : 8 + 2 * pair].reshape(128, 128)
            packed = own[d, 10 + pair].astype(F32)
            last = jnp.concatenate([packed, pltpu.roll(packed, 64, 1)], axis=0).astype(BF)
            moved = pltpu.roll(both.astype(F32), 64, 1).astype(BF)
            for group, q in enumerate((both, moved, last)):
                begin = e * 256 + pair * 128
                q_op[group, begin : begin + 128, :] = jnp.where(low_lane, q, q_tab[pair])

    contract = (((1,), (1,)), ((), ()))

    def mix(q, k_ref, v_ref, group, begin, end, state):
        for at_key in range(begin, end, 512):
            span = pl.ds(at_key, 512)
            scores = lax.dot_general(q, k_ref[group, span, :], contract, preferred_element_type=F32)
            top = jnp.broadcast_to(jnp.max(scores, axis=1, keepdims=True), (q.shape[0], 128))
            if state is not None:
                top = jnp.maximum(state[0], top)
            expo = jnp.exp(scores - jnp.concatenate([top] * 4, axis=1)).astype(BF)
            acc = jnp.dot(expo, v_ref[group, span, :], preferred_element_type=F32)
            if state is not None:
                acc += state[1] * jnp.exp(state[0] - top)
            state = (top, acc)
        return state

    def part(group, rows, begin, end, fresh):
        state = None if fresh else (tops[group, rows, :], sums[group, rows, :])
        return mix(q_op[group, rows, :], k_op, v_op, group, begin, end, state)

    def keep(group, rows, state):
        tops[group, rows, :], sums[group, rows, :] = state

    share(0, 0)
    share(0, 2)
    prepare_queries(0)
    for d in (2, 1):
        third[d, 0].wait_send()
        send(d, 1)
    third[3, 0].wait_send()
    send(3, 1)
    for d in (2, 1, 3):
        share(d, 0)
    for e in range(4):
        prepare_keys(e, 0)
    share_cross(0)
    found = [part(group, pl.ds(0, 256), 0, 1024, True) for group in range(3)]
    for group in range(3):
        keep(group, pl.ds(0, 256), found[group])
    for d in (2, 1, 3):
        send(d, 2)
    for e in range(1, 4):
        third[ARRIVAL[e], 1].wait_recv()
        prepare_queries(e)

    for group in range(3):
        rows = pl.ds(256, 768)
        keep(group, rows, part(group, rows, 0, 1024, True))

    prepare_keys(0, 2)
    for d in (2, 1, 3):
        share(d, 2)
    for d in (2, 1, 3):
        share_cross(d)
    for e in range(1, 4):
        prepare_keys(e, 2)

    for group in range(3):
        rows = pl.ds(0, 1024)
        keep(group, rows, part(group, rows, 1024, 2048, False))

    def finish(group, e, pair):
        acc = sums[group, e * 256 + pair * 128 : e * 256 + pair * 128 + 128, :]
        position = steps + (start_of(half, slot(ARRIVAL[e]), core) + 4 * pair)
        return jnp.where(position < length, acc / pltpu.roll(acc, 64, 1), 0.0)

    outs = []

    def give(turn):
        for e in (3, 1, 2, 0):
            d = ARRIVAL[e]
            low, high, middle = finish(0, e, 1 - turn), finish(2, e, 1 - turn), finish(1, e, turn)
            joined = jnp.where(low_lane, pltpu.roll(low, 64, 1), high)
            packed = jnp.where(low64, pltpu.roll(middle[0:64], 64, 1), middle[64:128])
            attn[d, 3 * turn : 3 * turn + 2] = joined.astype(BF).reshape(2, 64, 128)
            attn[d, 3 * turn + 2] = packed.astype(BF)
            src, dst = attn.at[d, pl.ds(3 * turn, 3)], back.at[cls, pl.ds(3 * turn, 3)]
            if d > 0:
                copy = remote(src, dst, out_send.at[turn, d - 1], out_recv.at[turn, d - 1], device(d))
            else:
                copy = pltpu.make_async_copy(src, dst, own_sem.at[turn])
            copy.start()
            outs.append(copy)

    give(0)
    for e in range(4):
        prepare_cross(e)

    for group in range(3):
        first = 128 * (group % 2)
        rows = [pl.ds(e * 256 + first, 128) for e in range(4)]
        q, top, acc = [jnp.concatenate([ref[group, r, :] for r in rows], axis=0) for ref in (q_op, tops, sums)]
        top, acc = mix(q, xk_op, xv_op, group, 0, 1024, (top, acc))
        for e in range(4):
            sums[group, rows[e], :] = acc[e * 128 : e * 128 + 128]

    give(1)
    for copy in outs:
        copy.wait()
    for d in range(4):
        if d > 0:
            third[d, 1].wait_send()
            third[d, 2].wait_send()
        sib_copies[d, 0].wait_send()
        sib_copies[d, 2].wait_send()
        x_copies[d].wait_send()
        xs_copies[d].wait_send()


def attend(recv, valid):
    vmem = pl.BlockSpec(memory_space=pltpu.VMEM)
    dma = pltpu.SemaphoreType.DMA
    return pl.pallas_call(
        attend_kernel,
        out_shape=jax.ShapeDtypeStruct((4, 6, 64, 128), BF),
        in_specs=[vmem, pl.BlockSpec(memory_space=pltpu.SMEM)],
        out_specs=pl.BlockSpec(memory_space=pltpu.HBM),
        scratch_shapes=[
            pltpu.VMEM((4, 18, 64, 128), BF),
            pltpu.VMEM((4, 12, 64, 128), BF),
            pltpu.VMEM((4, 6, 64, 128), BF),
            pltpu.VMEM((4, 6, 64, 128), BF),
            pltpu.VMEM((3, 18, 64, 128), BF),
            pltpu.VMEM((3, 1024, 128), BF),
            pltpu.VMEM((3, 2048, 128), BF),
            pltpu.VMEM((3, 2048, 128), BF),
            pltpu.VMEM((3, 1024, 128), BF),
            pltpu.VMEM((3, 1024, 128), BF),
            pltpu.VMEM((3, 1024, 128), F32),
            pltpu.VMEM((3, 1024, 128), F32),
            pltpu.VMEM((4, 6, 64, 128), BF),
            pltpu.VMEM((2, 128, 128), BF),
            pltpu.VMEM((3, 128, 128), BF),
            pltpu.VMEM((3, 128, 128), BF),
            dma((3, 3)),
            dma((3, 3)),
            dma((4, 2)),
            dma((4, 2)),
            dma((4,)),
            dma((4,)),
            dma((4,)),
            dma((4,)),
            dma((2, 3)),
            dma((2, 3)),
            dma((2,)),
        ],
        compiler_params=pltpu.CompilerParams(collective_id=1, has_side_effects=True, vmem_limit_bytes=VMEM_LIMIT),
        name="attend",
    )(recv, valid)


def output_kernel(rows_in, weight, out, mixed):
    @pl.when(pl.program_id(0) == 0)
    def _():
        for cls in range(4):
            w0, w1, w2 = [weight[(cls + 4 * g) * 64 : (cls + 4 * g + 1) * 64, :] for g in range(3)]
            zero = jnp.zeros((64, D), BF)
            w02 = jnp.concatenate([w0, w2], axis=0)
            ends = (jnp.concatenate([w1, zero], axis=0), jnp.concatenate([zero, w1], axis=0))
            rows = jnp.concatenate([rows_in[cls, i] for i in (3, 4, 0, 1)], axis=0)
            block = jnp.dot(rows, w02, preferred_element_type=F32)
            for a in range(4):
                middle = rows_in[cls, 2 if a < 2 else 5]
                total = block[a * 64 : a * 64 + 64] + jnp.dot(middle, ends[a % 2], preferred_element_type=F32)
                mixed[cls * 256 + a * 64 : cls * 256 + a * 64 + 64, :] = total.astype(BF)

    place = iota((256, ROWS), 0) + pl.program_id(0) * 256
    step = (place >> 2) & 3
    sorted_at = (place & 3) * 256 + (((step & 1) << 1) | (step >> 1)) * 64 + (place >> 4)
    one_hot = jnp.where(sorted_at == iota((256, ROWS), 1), 1.0, 0.0).astype(BF)
    out[...] = jnp.dot(one_hot, mixed[...], preferred_element_type=F32).astype(BF)


def output(rows_in, weight):
    return pl.pallas_call(
        output_kernel,
        grid=(4,),
        out_shape=jax.ShapeDtypeStruct((ROWS, D), BF),
        in_specs=[pl.BlockSpec((4, 6, 64, 128), lambda i: (0, 0, 0, 0)), pl.BlockSpec((D, D), lambda i: (0, 0))],
        out_specs=pl.BlockSpec((256, D), lambda i: (i, 0)),
        scratch_shapes=[pltpu.VMEM((ROWS, D), BF)],
        compiler_params=pltpu.CompilerParams(vmem_limit_bytes=32 * 1024 * 1024),
        name="output",
    )(rows_in, weight)


def local(tiles, destination, valid_len, in_weight, norm_gain, qkv_weight, out_weight):
    recv = project(tiles.reshape(CHUNK // BLOCK, PLACES, BLOCK, E), destination.reshape(8, 128), in_weight, norm_gain.reshape(D // 128, 128), qkv_weight)
    back = attend(recv.reshape(ROWS, WIDE), valid_len)
    return output(back, out_weight).reshape(1, ROWS, D)


def solution(mesh):
    in_specs = (P(("slide", "seq"), None), P(("slide", "seq")), P(), P(), P(), P(), P())
    return jax.shard_map(local, mesh=mesh, in_specs=in_specs, out_specs=P("slide", "seq", None), check_vma=False)
```

```python
import functools

import jax
import jax.numpy as jnp
from jax import lax
from jax.experimental import pallas as pl
from jax.experimental.pallas import tpu as pltpu
from jax.sharding import PartitionSpec as P

MESH = pl.DeviceIdType.MESH
SLIDES = 8
SEQ = 16
DEVICES = 128
ROWS = 1024
BLOCK = 8
E = 1536
D = 768
WIDE = 640
PLACES = 4
VMEM_LIMIT = 63 * 1024 * 1024
BF = jnp.bfloat16
F32 = jnp.float32
I32 = jnp.int32


def iota(shape, dim):
    return lax.broadcasted_iota(I32, shape, dim)


def pick_columns(qkv, place):
    rows = qkv.shape[0]
    lane = iota((rows, 128), 1)
    cls = place & 3
    high = cls >= 2
    odd = (cls & 1) == 1
    low_lane = lane < 64

    def head(kind, group):
        at = kind * D + group * 256
        return jnp.where(high, qkv[:, at + 128 : at + 256], qkv[:, at : at + 128])

    def pair(left, right):
        moved = pltpu.roll(jnp.where(odd, left, right), 64, 1)
        return jnp.where(low_lane == odd, moved, jnp.where(odd, right, left))

    step = (place >> 2) & 3
    sorted_at = cls * 256 + (((step & 1) << 1) | (step >> 1)) * 64 + (place >> 4)
    ids = jnp.where(lane == 64, sorted_at >> 7, jnp.where(lane == 65, sorted_at & 127, 0)).astype(F32)
    q2 = head(0, 2) * 0.125
    q2 = jnp.where(odd, pltpu.roll(q2, 64, 1), q2)
    return (
        pair(head(0, 0) * 0.125, head(0, 1) * 0.125),
        jnp.where(low_lane, q2, ids),
        pair(head(1, 0), head(2, 0)),
        pair(head(1, 2), head(2, 2)),
        pair(head(1, 1), head(2, 1)),
    )


def project_kernel(tiles, dest, w_in, gain, w_qkv, recv, tiles_v, w_in_v, w_qkv_v, dest_v, gain_v, send, load_sem, send_sem, recv_sem, own_sem):
    slide = lax.axis_index("slide")
    seq = lax.axis_index("seq")
    me = slide * SEQ + seq
    across = seq // PLACES
    place_me = lax.rem(seq, PLACES)

    def place_at(step):
        return lax.rem(place_me + step, PLACES)

    loads = [
        pltpu.make_async_copy(w_in, w_in_v, load_sem.at[0]),
        pltpu.make_async_copy(w_qkv, w_qkv_v, load_sem.at[1]),
        pltpu.make_async_copy(dest, dest_v, load_sem.at[2]),
        pltpu.make_async_copy(gain, gain_v, load_sem.at[3]),
    ]
    for step in range(PLACES):
        loads.append(pltpu.make_async_copy(tiles.at[:, :, :, place_at(step)], tiles_v.at[step], load_sem.at[4 + step]))
    for index in (0, 4, 2, 3, 1, 5, 6, 7):
        loads[index].start()

    barrier = pltpu.get_barrier_semaphore()

    @pl.loop(1, DEVICES)
    def _(i):
        other = lax.rem(me + i, DEVICES)
        pl.semaphore_signal(barrier, inc=1, device_id=(other // SEQ, lax.rem(other, SEQ)), device_id_type=MESH)

    def wait_first(step, load):
        if step == 0:
            load.wait()

    for step in range(PLACES + 1):
        turn = max(step - 1, 0)
        place = place_at(turn)
        across_low = lax.rem(across + step, 2) if step < 2 else None
        blocks = DEVICES // PLACES // (2 if step < 2 else 1)
        rows = blocks * BLOCK
        wait_first(step, loads[0])
        if step != 1:
            loads[4 + turn].wait()
        x = tiles_v[turn, :, :, across_low] if step < 2 else tiles_v[turn]
        proj = jnp.dot(x.reshape(rows, E), w_in_v[...], preferred_element_type=F32).astype(BF).astype(F32)
        mean = jnp.mean(proj, axis=-1, keepdims=True)
        centred = proj - mean
        var = jnp.mean(centred * centred, axis=-1, keepdims=True)
        wait_first(step, loads[3])
        gains = jnp.concatenate([gain_v[i : i + 1, :] for i in range(D // 128)], axis=1)
        normed = (centred * lax.rsqrt(var + 1e-05) * gains).astype(BF)
        wait_first(step, loads[1])
        qkv = jnp.dot(normed, w_qkv_v[...], preferred_element_type=F32)
        wait_first(step, loads[2])
        lines = (dest_v[...] & (ROWS - 1)).astype(F32)
        lines = jnp.broadcast_to(lines.reshape(8, 1, 128), (8, rows // 8, 128)).reshape(rows, 128)
        r = iota((rows, 128), 0)
        to = (r >> 3) & 3 if step >= 2 else ((r >> 3) & 1) * 2 + across_low
        wanted = to * 32 + place * 8 + (r & 7)
        position = jnp.sum(jnp.where(iota((rows, 128), 1) == wanted, lines, 0.0), axis=1, keepdims=True).astype(I32)
        for index, block in enumerate(pick_columns(qkv, position)):
            lanes = pl.ds(index * 128, 128)
            if step < 2:
                send[:, :, across_low, place, :, lanes] = block.reshape(SLIDES, 2, BLOCK, 128).astype(BF)
            else:
                send[:, :, :, place, :, lanes] = block.reshape(SLIDES, 2, 2, BLOCK, 128).astype(BF)
        if step == 0:
            pl.semaphore_wait(barrier, DEVICES - 1)

        @pl.loop(0, blocks)
        def _(i):
            to_slide = lax.rem(slide + i, SLIDES)
            to_across = lax.rem(across + (i // SLIDES * 2 + step if step < 2 else i // SLIDES), 4)

            @pl.when((to_slide != slide) | (to_across != across) | (place != place_me))
            def _():
                pltpu.make_async_remote_copy(
                    src_ref=send.at[to_slide, to_across // 2, lax.rem(to_across, 2), place],
                    dst_ref=recv.at[me],
                    send_sem=send_sem,
                    recv_sem=recv_sem,
                    device_id=(to_slide, to_across * PLACES + place),
                    device_id_type=MESH,
                ).start()

    own = pltpu.make_async_copy(send.at[slide, across // 2, lax.rem(across, 2), place_me], recv.at[me], own_sem)
    own.start()
    own.wait()
    rest = pl.ds(0, DEVICES - 1)
    pltpu.make_async_copy(recv.at[rest], recv.at[rest], send_sem).wait()
    pltpu.make_async_copy(recv.at[rest], recv.at[rest], recv_sem).wait()


def project(tiles, dest, w_in, gain, w_qkv):
    hbm = pl.BlockSpec(memory_space=pltpu.HBM)
    return pl.pallas_call(
        project_kernel,
        out_shape=jax.ShapeDtypeStruct((DEVICES, BLOCK, WIDE), BF),
        in_specs=[hbm] * 5,
        out_specs=hbm,
        scratch_shapes=[
            pltpu.VMEM((PLACES, SLIDES, 2, 2, BLOCK, E), BF),
            pltpu.VMEM((E, D), BF),
            pltpu.VMEM((D, 3 * D), BF),
            pltpu.VMEM((8, 128), I32),
            pltpu.VMEM((D // 128, 128), F32),
            pltpu.VMEM((SLIDES, 2, 2, PLACES, BLOCK, WIDE), BF),
            pltpu.SemaphoreType.DMA((4 + PLACES,)),
            pltpu.SemaphoreType.DMA,
            pltpu.SemaphoreType.DMA,
            pltpu.SemaphoreType.DMA,
        ],
        compiler_params=pltpu.CompilerParams(collective_id=0, has_side_effects=True, vmem_limit_bytes=VMEM_LIMIT),
        name="project_send",
    )(tiles, dest, w_in, gain, w_qkv)


ARRIVAL = (0, 2, 1, 3)
PAIR_OF = ((0, 1), (2, 3), (1, 0))
LN2 = (0.69140625, 0.0017409306)
LN3 = (1.1015625, -0.0029502113)
KV_AT = (2, 4, 3)


def key_table(group, inner):
    lane = iota((128, 128), 1)
    key = iota((128, 128), 0) // 64 + 2 * (group % 2)
    third, second = PAIR_OF[group]
    query = jnp.where(lane < 69, lane - 65, lane - 69)
    used = (lane >= 65) & (lane < 73)
    twice = used & ((query == third) | (query == second))
    thrice = used & (query == third) & (key == third)
    first = lane < 69
    ln2 = jnp.where(first, LN2[0], LN2[1])
    ln3 = jnp.where(first, LN3[0], LN3[1])
    if inner:
        return jnp.where(thrice, ln3, jnp.where(twice, ln2, 0.0))
    return jnp.where(thrice, ln2, 0.0)


def attend_kernel(
    recv, valid, back, own, sib, x_own, x_sib, stage, q_op, k_op, v_op, xk_op, xv_op, tops, sums, attn, q_tab, k_tab, x_tab,
    send_sem, recv_sem, sib_send, sib_recv, x_send, x_recv, xs_send, xs_recv, out_send, out_recv, own_sem,
):
    slide = lax.axis_index("slide")
    seq = lax.axis_index("seq")
    half = seq // 8
    row = lax.rem(seq // 4, 2)
    col = lax.rem(seq // 2, 2)
    core = lax.rem(seq, 2)

    def slot(d):
        return 2 * lax.rem(row + d // 2, 2) + lax.rem(col + d % 2, 2)

    def cross_slot(d):
        return 2 * lax.rem(1 - row + d // 2, 2) + lax.rem(col + d % 2, 2)

    def cls_of(d):
        return 2 * lax.rem(row + d // 2 + half, 2) + lax.rem(col + d % 2, 2)

    def device(d):
        return (slide, half * 8 + slot(d) * 2 + core)

    sibling = (slide, seq + 1 - 2 * core)
    cross = (slide, (1 - half) * 8 + cross_slot(0) * 2 + core)
    partners = [device(1), device(2), device(3), sibling, cross]

    barrier = pltpu.get_barrier_semaphore()
    for other in partners:
        pl.semaphore_signal(barrier, inc=1, device_id=other, device_id_type=MESH)

    rows_in = recv[...]
    lane8 = iota((8, 128), 1)
    weigh = jnp.where(lane8 == 64, 128.0, jnp.where(lane8 == 65, 1.0, 0.0)).astype(BF)
    at = lax.dot_general(weigh, rows_in[:, 128:256], (((1,), (1,)), ((), ())), preferred_element_type=F32)
    at = at[0:1].astype(I32)
    low64 = iota((64, 128), 1) < 64

    def sort_class(cls, ref):
        hit = (at - cls * 256) == iota((256, ROWS), 0)
        one_hot = jnp.where(hit, 1.0, 0.0).astype(BF)
        found = jnp.dot(one_hot, rows_in, preferred_element_type=F32)

        def tile(a, t):
            return found[a * 64 : a * 64 + 64, t * 128 : t * 128 + 128]

        for group in range(3):
            for i in range(4):
                ref[6 * group + i] = tile((2 * (group % 2) + i) % 4, KV_AT[group]).astype(BF)
            for pair in range(2):
                even, odd = tile(2 * pair, group // 2), tile(2 * pair + 1, group // 2)
                if group == 1:
                    even = pltpu.roll(even, 64, 1)
                else:
                    odd = pltpu.roll(odd, 64, 1)
                ref[6 * group + 4 + pair] = jnp.where(low64, even, odd).astype(BF)

    def remote(src, dst, send, recv_, to):
        return pltpu.make_async_remote_copy(
            src_ref=src, dst_ref=dst, send_sem=send, recv_sem=recv_, device_id=to, device_id_type=MESH
        )

    sends = {}

    def send(d, group):
        part = pl.ds(6 * group, 6)
        copy = remote(
            stage.at[d - 1, part], own.at[d, part], send_sem.at[d - 1, group], recv_sem.at[d - 1, group], device(d)
        )
        copy.start()
        sends[d, group] = copy

    for order, d in enumerate(ARRIVAL[1:]):
        sort_class(cls_of(d), stage.at[d - 1])
        if order == 0:
            pl.semaphore_wait(barrier, len(partners))
        send(d, 0)
    for group in range(1, 3):
        for d in ARRIVAL[1:]:
            send(d, group)
    sort_class(cls_of(0), own.at[0])

    sib_copies, x_copies, xs_copies = {}, {}, {}

    def share(d, group):
        if d > 0:
            sends[d, group].wait_recv()
        sib_copies[d, group] = remote(
            own.at[d, pl.ds(6 * group, 4)], sib.at[d, pl.ds(4 * group, 4)], sib_send.at[d, group], sib_recv.at[d, group], sibling
        )
        sib_copies[d, group].start()
        x_copies[d, group] = remote(
            own.at[d, pl.ds(6 * group, 2)], x_own.at[d, pl.ds(2 * group, 2)], x_send.at[d, group], x_recv.at[d, group], cross
        )
        x_copies[d, group].start()

    def share_cross(d, group):
        x_copies[d, group].wait_recv()
        part = pl.ds(2 * group, 2)
        xs_copies[d, group] = remote(x_own.at[d, part], x_sib.at[d, part], xs_send.at[d, group], xs_recv.at[d, group], sibling)
        xs_copies[d, group].start()

    cls = cls_of(0)
    length = valid[slide]
    lane = iota((128, 128), 1)
    low_lane = lane < 64
    line = iota((128, 128), 0)
    steps = lax.rem(line, 64) * 16 + (line // 64) * 8

    def start_of(half_, slot_, core_):
        return half_ * 8192 + slot_ * 2048 + core_ * 1024 + cls

    for pair in range(2):
        residue = line // 64 + 2 * pair
        ones = jnp.where((lane == 64) | (lane == 65 + residue) | (lane == 69 + residue), 1.0, 0.0)
        q_tab[pair] = ones.astype(BF)
    for group in range(3):
        k_tab[group] = key_table(group, True).astype(BF)
        x_tab[group] = key_table(group, False).astype(BF)

    def keys(k_ref, v_ref, group, at_row, block, position, table):
        block = block.reshape(128, 128)
        bias = jnp.where((lane == 64) & (position >= length), jnp.full_like(block, -1e30), table)
        k_ref[group, at_row : at_row + 128, :] = jnp.where(low_lane, block, bias)
        v_ref[group, at_row : at_row + 128, :] = jnp.where(low_lane, jnp.ones_like(block), block)

    def prepare(e, group):
        d = ARRIVAL[e]
        for pair in range(2):
            packed = own[d, 6 * group + 4 + pair].astype(F32)
            q = jnp.concatenate([packed, pltpu.roll(packed, 64, 1)], axis=0).astype(BF)
            begin = e * 256 + pair * 128
            q_op[group, begin : begin + 128, :] = jnp.where(low_lane, q, q_tab[pair])
        sib_copies[d, group].wait_recv()
        for source, core_, first in ((own, core, 6 * group), (sib, 1 - core, 4 * group)):
            for rest in range(2):
                at_row = e * 512 + rest * 256 + (0 if source is own else 128)
                position = steps + (start_of(half, slot(d), core_) + 4 * ((group + rest) % 2))
                table = k_tab[group] if rest == 0 else jnp.zeros((128, 128), BF)
                at_tile = first + 2 * rest
                keys(k_op, v_op, group, at_row, source[d, at_tile : at_tile + 2], position, table)

    def prepare_cross(e, group):
        d = ARRIVAL[e]
        xs_copies[d, group].wait_recv()
        for source, core_ in ((x_own, core), (x_sib, 1 - core)):
            at_row = e * 256 + (0 if source is x_own else 128)
            position = steps + (start_of(1 - half, cross_slot(d), core_) + 4 * (group % 2))
            keys(xk_op, xv_op, group, at_row, source[d, 2 * group : 2 * group + 2], position, x_tab[group])

    contract = (((1,), (1,)), ((), ()))

    def mix(q, k_ref, v_ref, group, spans, state):
        for begin, end in spans:
            span = pl.ds(begin, end - begin)
            scores = lax.dot_general(q, k_ref[group, span, :], contract, preferred_element_type=F32)
            top = jnp.broadcast_to(jnp.max(scores, axis=1, keepdims=True), (q.shape[0], 128))
            if state is not None:
                top = jnp.maximum(state[0], top)
            expo = jnp.exp(scores - jnp.concatenate([top] * ((end - begin) // 128), axis=1)).astype(BF)
            acc = jnp.dot(expo, v_ref[group, span, :], preferred_element_type=F32)
            if state is not None:
                acc += state[1] * jnp.exp(state[0] - top)
            state = (top, acc)
        return state

    outs = []

    def give(e, group):
        d = ARRIVAL[e]
        for pair in range(2):
            acc = sums[group, e * 256 + pair * 128 : e * 256 + pair * 128 + 128, :]
            position = steps + (start_of(half, slot(d), core) + 4 * pair)
            out = jnp.where(position < length, acc / pltpu.roll(acc, 64, 1), 0.0)
            attn[d, 2 * group + pair] = jnp.where(low64, pltpu.roll(out[0:64], 64, 1), out[64:128]).astype(BF)
        part = pl.ds(2 * group, 2)
        src, dst = attn.at[d, part], back.at[cls, part]
        if d > 0:
            copy = remote(src, dst, out_send.at[group, d - 1], out_recv.at[group, d - 1], device(d))
        else:
            copy = pltpu.make_async_copy(src, dst, own_sem.at[group])
        copy.start()
        outs.append(copy)

    def attend_half(group):
        for e in range(4):
            prepare(e, group)
        spans = [(begin, begin + 512) for begin in range(0, 2048, 512)]
        tops[group], sums[group] = mix(q_op[group], k_op, v_op, group, spans, None)

    def attend_cross(group):
        for e in range(4):
            prepare_cross(e, group)
        first = 128 * (group % 2)
        rows = [pl.ds(e * 256 + first, 128) for e in range(4)]
        q, top, acc = [jnp.concatenate([ref[group, r, :] for r in rows], axis=0) for ref in (q_op, tops, sums)]
        _, acc = mix(q, xk_op, xv_op, group, ((0, 512), (512, 1024)), (top, acc))
        for e in range(4):
            sums[group, rows[e], :] = acc[e * 128 : e * 128 + 128]
        for e in (3, 1, 2, 0):
            give(e, group)

    for group in range(3):
        share(0, group)
    for d in ARRIVAL[1:]:
        share(d, 0)
    attend_half(0)
    for d in ARRIVAL[1:]:
        share(d, 1)
    for d in ARRIVAL:
        share_cross(d, 0)
    attend_half(1)
    for d in ARRIVAL[1:]:
        share(d, 2)
    for d in ARRIVAL:
        share_cross(d, 1)
    attend_cross(0)
    attend_half(2)
    for d in ARRIVAL:
        share_cross(d, 2)
    attend_cross(1)
    attend_cross(2)
    for copy in outs:
        copy.wait()
    for group in range(3):
        for d in range(4):
            if d > 0:
                sends[d, group].wait_send()
            sib_copies[d, group].wait_send()
            x_copies[d, group].wait_send()
            xs_copies[d, group].wait_send()


def attend(recv, valid):
    vmem = pl.BlockSpec(memory_space=pltpu.VMEM)
    dma = pltpu.SemaphoreType.DMA
    return pl.pallas_call(
        attend_kernel,
        out_shape=jax.ShapeDtypeStruct((4, 6, 64, 128), BF),
        in_specs=[vmem, pl.BlockSpec(memory_space=pltpu.SMEM)],
        out_specs=pl.BlockSpec(memory_space=pltpu.HBM),
        scratch_shapes=[
            pltpu.VMEM((4, 18, 64, 128), BF),
            pltpu.VMEM((4, 12, 64, 128), BF),
            pltpu.VMEM((4, 6, 64, 128), BF),
            pltpu.VMEM((4, 6, 64, 128), BF),
            pltpu.VMEM((3, 18, 64, 128), BF),
            pltpu.VMEM((3, 1024, 128), BF),
            pltpu.VMEM((3, 2048, 128), BF),
            pltpu.VMEM((3, 2048, 128), BF),
            pltpu.VMEM((3, 1024, 128), BF),
            pltpu.VMEM((3, 1024, 128), BF),
            pltpu.VMEM((3, 1024, 128), F32),
            pltpu.VMEM((3, 1024, 128), F32),
            pltpu.VMEM((4, 6, 64, 128), BF),
            pltpu.VMEM((2, 128, 128), BF),
            pltpu.VMEM((3, 128, 128), BF),
            pltpu.VMEM((3, 128, 128), BF),
            dma((3, 3)),
            dma((3, 3)),
            dma((4, 3)),
            dma((4, 3)),
            dma((4, 3)),
            dma((4, 3)),
            dma((4, 3)),
            dma((4, 3)),
            dma((3, 3)),
            dma((3, 3)),
            dma((3,)),
        ],
        compiler_params=pltpu.CompilerParams(collective_id=1, has_side_effects=True, vmem_limit_bytes=VMEM_LIMIT),
        name="attend",
    )(recv, valid)


def output_kernel(rows_hbm, weight_hbm, out, rows_in, weight, spread, packed, load_sem, out_sem):
    loads = [
        pltpu.make_async_copy(weight_hbm, weight, load_sem.at[0]),
        pltpu.make_async_copy(rows_hbm, rows_in, load_sem.at[1]),
    ]
    for copy in loads:
        copy.start()
    for copy in loads:
        copy.wait()
    low = iota((64, 128), 1) < 64
    for cls in range(4):
        heads = [weight[(cls + 4 * g) * 64 : (cls + 4 * g + 1) * 64, :] for g in range(3)]
        wide = jnp.concatenate([w for w in heads for _ in range(2)], axis=0)
        columns = []
        for g in range(3):
            tiles = [rows_in[cls, 2 * g + a // 2] for a in range(4)]
            masked = [jnp.where(low == (a % 2 == 0), tile, jnp.zeros_like(tile)) for a, tile in enumerate(tiles)]
            columns.append(jnp.concatenate(masked, axis=0))
        rows = jnp.concatenate(columns, axis=1)
        total = jnp.dot(rows, wide, preferred_element_type=F32)
        for a in range(4):
            residue = cls + (a % 2) * 8 + (a // 2) * 4
            for t in range(D // 128):
                spread[t, pl.ds(residue, 64, stride=16), :] = total[a * 64 : a * 64 + 64, t * 128 : t * 128 + 128]
    copies = []
    for index in range(4):
        span = pl.ds(index * 256, 256)
        for t in range(D // 128):
            packed[span, t * 128 : t * 128 + 128] = spread[t, span, :].astype(BF)
        copy = pltpu.make_async_copy(packed.at[span], out.at[span], out_sem.at[index])
        copy.start()
        copies.append(copy)
    for copy in copies:
        copy.wait()


def output(rows_in, weight):
    hbm = pl.BlockSpec(memory_space=pltpu.HBM)
    return pl.pallas_call(
        output_kernel,
        out_shape=jax.ShapeDtypeStruct((ROWS, D), BF),
        in_specs=[hbm, hbm],
        out_specs=hbm,
        scratch_shapes=[
            pltpu.VMEM((4, 6, 64, 128), BF),
            pltpu.VMEM((D, D), BF),
            pltpu.VMEM((D // 128, ROWS, 128), F32),
            pltpu.VMEM((ROWS, D), BF),
            pltpu.SemaphoreType.DMA((2,)),
            pltpu.SemaphoreType.DMA((4,)),
        ],
        compiler_params=pltpu.CompilerParams(vmem_limit_bytes=VMEM_LIMIT),
        name="output",
    )(rows_in, weight)


def local(tiles, destination, valid_len, in_weight, norm_gain, qkv_weight, out_weight):
    recv = project(tiles.reshape(SLIDES, 2, 2, PLACES, BLOCK, E), destination.reshape(8, 128), in_weight, norm_gain.reshape(D // 128, 128), qkv_weight)
    back = attend(recv.reshape(ROWS, WIDE), valid_len)
    return output(back, out_weight).reshape(1, ROWS, D)


def solution(mesh):
    in_specs = (P(("slide", "seq"), None), P(("slide", "seq")), P(), P(), P(), P(), P())
    return jax.shard_map(local, mesh=mesh, in_specs=in_specs, out_specs=P("slide", "seq", None), check_vma=False)
```

```python
import functools

import jax
import jax.numpy as jnp
from jax import lax
from jax.experimental import pallas as pl
from jax.experimental.pallas import tpu as pltpu
from jax.sharding import PartitionSpec as P

MESH = pl.DeviceIdType.MESH
SLIDES = 8
SEQ = 16
DEVICES = 128
ROWS = 1024
BLOCK = 8
E = 1536
D = 768
PLACES = 4
CHUNK = 256
VMEM_LIMIT = 63 * 1024 * 1024
BF = jnp.bfloat16
F32 = jnp.float32
I32 = jnp.int32


def iota(shape, dim):
    return lax.broadcasted_iota(I32, shape, dim)


WIDTHS = (256, 256, 128)
NEEDS = (((1, 0), (2, 0), (0, 0)), ((1, 1), (2, 1), (0, 1), (0, 2)), ((1, 2), (2, 2)))


def pick_columns(turn, columns, place):
    rows = place.shape[0]
    lane = iota((rows, 128), 1)
    cls = place & 3
    high = cls >= 2
    odd = (cls & 1) == 1
    low_lane = lane < 64
    heads = [jnp.where(high, block[:, 128:256], block[:, 0:128]) for block in columns]

    def pair(left, right):
        moved = pltpu.roll(jnp.where(odd, left, right), 64, 1)
        return jnp.where(low_lane == odd, moved, jnp.where(odd, right, left))

    picked = [pair(heads[0], heads[1])]
    if turn == 0:
        step = (place >> 2) & 3
        sorted_at = cls * 256 + (((step & 1) << 1) | (step >> 1)) * 64 + (place >> 4)
        ids = jnp.where(lane == 64, sorted_at >> 7, jnp.where(lane == 65, sorted_at & 127, 0)).astype(F32)
        q = heads[2] * 0.125
        picked.append(jnp.where(low_lane, jnp.where(odd, pltpu.roll(q, 64, 1), q), ids))
    if turn == 1:
        picked.append(pair(heads[2] * 0.125, heads[3] * 0.125))
    return picked


ARRIVAL = (0, 2, 1, 3)
PAIR_OF = ((0, 1), (2, 3), (1, 0))
LN2 = (0.69140625, 0.0017409306)
LN3 = (1.1015625, -0.0029502113)

def key_table(group, inner):
    lane = iota((128, 128), 1)
    key = iota((128, 128), 0) // 64 + 2 * (group % 2)
    third, second = PAIR_OF[group]
    query = jnp.where(lane < 69, lane - 65, lane - 69)
    used = (lane >= 65) & (lane < 73)
    twice = used & ((query == third) | (query == second))
    thrice = used & (query == third) & (key == third)
    first = lane < 69
    ln2 = jnp.where(first, LN2[0], LN2[1])
    ln3 = jnp.where(first, LN3[0], LN3[1])
    if inner:
        return jnp.where(thrice, ln3, jnp.where(twice, ln2, 0.0))
    return jnp.where(thrice, ln2, 0.0)


def layer_kernel(
    tiles, dest, w_in, gain, w_qkv, valid, back,
    tiles_v, w_in_v, w_qkv_v, dest_v, gain_v, normed_v, out0, out1, out2, in0, in1, in2, hot,
    own, sib, x_own, x_sib, stage, q_op, k_op, v_op, xk_op, xv_op, tops, sums, attn, q_tab, k_tab, x_tab,
    load_sem, go_sem, come_sem, stay_sem,
    send_sem, recv_sem, sib_send, sib_recv, x_send, x_recv, xs_send, xs_recv, out_send, out_recv, own_sem,
):
    slide = lax.axis_index("slide")
    seq = lax.axis_index("seq")
    me = slide * SEQ + seq
    across = seq // PLACES
    place_me = lax.rem(seq, PLACES)
    half = seq // 8
    row = lax.rem(seq // 4, 2)
    col = lax.rem(seq // 2, 2)
    core = lax.rem(seq, 2)
    leaving, coming = (out0, out1, out2), (in0, in1, in2)

    def place_at(step):
        return lax.rem(place_me + step, PLACES)

    loads = [
        pltpu.make_async_copy(w_in, w_in_v, load_sem.at[0]),
        pltpu.make_async_copy(w_qkv, w_qkv_v, load_sem.at[1]),
        pltpu.make_async_copy(dest, dest_v, load_sem.at[2]),
        pltpu.make_async_copy(gain, gain_v, load_sem.at[3]),
    ]
    for step in range(PLACES):
        loads.append(pltpu.make_async_copy(tiles.at[:, place_at(step)], tiles_v.at[step], load_sem.at[4 + step]))
    for index in (0, 4, 2, 3, 1, 5, 6, 7):
        loads[index].start()

    barrier = pltpu.get_barrier_semaphore()

    @pl.loop(1, DEVICES)
    def _(i):
        other = lax.rem(me + i, DEVICES)
        pl.semaphore_signal(barrier, inc=1, device_id=(other // SEQ, lax.rem(other, SEQ)), device_id_type=MESH)

    def project(step):
        if step == 0:
            loads[0].wait()
            loads[3].wait()
        loads[4 + step].wait()
        x = tiles_v[step].reshape(CHUNK, E)
        proj = jnp.dot(x, w_in_v[...], preferred_element_type=F32).astype(BF).astype(F32)
        mean = jnp.mean(proj, axis=-1, keepdims=True)
        centred = proj - mean
        var = jnp.mean(centred * centred, axis=-1, keepdims=True)
        gains = jnp.concatenate([gain_v[i : i + 1, :] for i in range(D // 128)], axis=1)
        normed_v[step] = (centred * lax.rsqrt(var + 1e-05) * gains).astype(BF)

    def fill(step, turn):
        place = place_at(step)
        normed = normed_v[step]
        columns = [
            jnp.dot(normed, w_qkv_v[:, kind * D + group * 256 : kind * D + group * 256 + 256], preferred_element_type=F32)
            for kind, group in NEEDS[turn]
        ]
        lines = (dest_v[...] & (ROWS - 1)).astype(F32)
        lines = jnp.broadcast_to(lines.reshape(8, 1, 128), (8, 32, 128)).reshape(CHUNK, 128)
        r = iota((CHUNK, 128), 0)
        wanted = ((r >> 3) & 3) * 32 + place * 8 + (r & 7)
        position = jnp.sum(jnp.where(iota((CHUNK, 128), 1) == wanted, lines, 0.0), axis=1, keepdims=True).astype(I32)
        for index, block in enumerate(pick_columns(turn, columns, position)):
            lanes = pl.ds(index * 128, 128)
            leaving[turn][:, place, :, lanes] = block.reshape(CHUNK // BLOCK, BLOCK, 128).astype(BF)

    def leave(step, turn):
        place = place_at(step)

        @pl.loop(0, CHUNK // BLOCK)
        def _(i):
            to_slide = lax.rem(slide + i, SLIDES)
            to_across = lax.rem(across + i // SLIDES, 4)

            @pl.when((to_slide != slide) | (to_across != across) | (place != place_me))
            def _():
                pltpu.make_async_remote_copy(
                    src_ref=leaving[turn].at[to_slide * 4 + to_across, place],
                    dst_ref=coming[turn].at[me],
                    send_sem=go_sem.at[turn],
                    recv_sem=come_sem.at[turn],
                    device_id=(to_slide, to_across * PLACES + place),
                    device_id_type=MESH,
                ).start()

    def stay(turn):
        copy = pltpu.make_async_copy(
            leaving[turn].at[slide * 4 + across, place_me], coming[turn].at[me], stay_sem.at[turn]
        )
        copy.start()
        copy.wait()

    others = pl.ds(0, DEVICES - 1)

    def arrived(turn):
        part = coming[turn].at[others]
        pltpu.make_async_copy(part, part, come_sem.at[turn]).wait()

    def left(turn):
        part = coming[turn].at[others]
        pltpu.make_async_copy(part, part, go_sem.at[turn]).wait()

    def slot(d):
        return 2 * lax.rem(row + d // 2, 2) + lax.rem(col + d % 2, 2)

    def cross_slot(d):
        return 2 * lax.rem(1 - row + d // 2, 2) + lax.rem(col + d % 2, 2)

    def cls_of(d):
        return 2 * lax.rem(row + d // 2 + half, 2) + lax.rem(col + d % 2, 2)

    def device(d):
        return (slide, half * 8 + slot(d) * 2 + core)

    sibling = (slide, seq + 1 - 2 * core)
    cross = (slide, (1 - half) * 8 + cross_slot(0) * 2 + core)

    low64 = iota((64, 128), 1) < 64

    def target(d):
        return own.at[0] if d == 0 else stage.at[d - 1]

    def mark():
        lane8 = iota((8, 128), 1)
        weigh = jnp.where(lane8 == 64, 128.0, jnp.where(lane8 == 65, 1.0, 0.0)).astype(BF)
        ids = in0[...].reshape(ROWS, WIDTHS[0])[:, 128:256]
        at = lax.dot_general(weigh, ids, (((1,), (1,)), ((), ())), preferred_element_type=F32)
        at = at[0:1].astype(I32)
        for d in range(4):
            hit = (at - cls_of(d) * 256) == iota((256, ROWS), 0)
            hot[d] = jnp.where(hit, 1.0, 0.0).astype(BF)

    def sort(d, turn):
        rows_in = coming[turn][...].reshape(ROWS, WIDTHS[turn])
        found = jnp.dot(hot[d], rows_in, preferred_element_type=F32)
        ref = target(d)

        def tile(a, t):
            return found[a * 64 : a * 64 + 64, t * 128 : t * 128 + 128]

        for i in range(4):
            ref[6 * turn + i] = tile((2 * (turn % 2) + i) % 4, 0).astype(BF)
        for pair in range(2):
            if turn < 2:
                even, odd = tile(2 * pair, 1), tile(2 * pair + 1, 1)
                ref[6 * turn + 4 + pair] = jnp.where(low64, even, pltpu.roll(odd, 64, 1)).astype(BF)
            if turn == 1:
                ref[16 + pair] = jnp.where(low64, pltpu.roll(even, 64, 1), odd).astype(BF)

    def remote(src, dst, send, recv_, to):
        return pltpu.make_async_remote_copy(
            src_ref=src, dst_ref=dst, send_sem=send, recv_sem=recv_, device_id=to, device_id_type=MESH
        )

    sends = {}

    def send(d, group):
        part = pl.ds(6 * group, 6)
        copy = remote(
            stage.at[d - 1, part], own.at[d, part], send_sem.at[d - 1, group], recv_sem.at[d - 1, group], device(d)
        )
        copy.start()
        sends[d, group] = copy

    sib_copies, x_copies, xs_copies = {}, {}, {}

    def share(d, group):
        if d > 0:
            sends[d, group].wait_recv()
        sib_copies[d, group] = remote(
            own.at[d, pl.ds(6 * group, 4)], sib.at[d, pl.ds(4 * group, 4)], sib_send.at[d, group], sib_recv.at[d, group], sibling
        )
        sib_copies[d, group].start()
        x_copies[d, group] = remote(
            own.at[d, pl.ds(6 * group, 2)], x_own.at[d, pl.ds(2 * group, 2)], x_send.at[d, group], x_recv.at[d, group], cross
        )
        x_copies[d, group].start()

    def share_cross(d, group):
        x_copies[d, group].wait_recv()
        part = pl.ds(2 * group, 2)
        xs_copies[d, group] = remote(x_own.at[d, part], x_sib.at[d, part], xs_send.at[d, group], xs_recv.at[d, group], sibling)
        xs_copies[d, group].start()

    cls = cls_of(0)
    length = valid[slide]
    lane = iota((128, 128), 1)
    low_lane = lane < 64
    line = iota((128, 128), 0)
    steps = lax.rem(line, 64) * 16 + (line // 64) * 8

    def start_of(half_, slot_, core_):
        return half_ * 8192 + slot_ * 2048 + core_ * 1024 + cls

    for pair in range(2):
        residue = line // 64 + 2 * pair
        ones = jnp.where((lane == 64) | (lane == 65 + residue) | (lane == 69 + residue), 1.0, 0.0)
        q_tab[pair] = ones.astype(BF)
    for group in range(3):
        k_tab[group] = key_table(group, True).astype(BF)
        x_tab[group] = key_table(group, False).astype(BF)

    def keys(k_ref, v_ref, group, at_row, block, position, table):
        block = block.reshape(128, 128)
        bias = jnp.where((lane == 64) & (position >= length), jnp.full_like(block, -1e30), table)
        k_ref[group, at_row : at_row + 128, :] = jnp.where(low_lane, block, bias)
        v_ref[group, at_row : at_row + 128, :] = jnp.where(low_lane, jnp.ones_like(block), block)

    def prepare(e, group):
        d = ARRIVAL[e]
        for pair in range(2):
            packed = own[d, 6 * group + 4 + pair].astype(F32)
            q = jnp.concatenate([packed, pltpu.roll(packed, 64, 1)], axis=0).astype(BF)
            begin = e * 256 + pair * 128
            q_op[group, begin : begin + 128, :] = jnp.where(low_lane, q, q_tab[pair])
        sib_copies[d, group].wait_recv()
        for source, core_, first in ((own, core, 6 * group), (sib, 1 - core, 4 * group)):
            for rest in range(2):
                at_row = e * 512 + rest * 256 + (0 if source is own else 128)
                position = steps + (start_of(half, slot(d), core_) + 4 * ((group + rest) % 2))
                table = k_tab[group] if rest == 0 else jnp.zeros((128, 128), BF)
                at_tile = first + 2 * rest
                keys(k_op, v_op, group, at_row, source[d, at_tile : at_tile + 2], position, table)

    def prepare_cross(e, group):
        d = ARRIVAL[e]
        xs_copies[d, group].wait_recv()
        for source, core_ in ((x_own, core), (x_sib, 1 - core)):
            at_row = e * 256 + (0 if source is x_own else 128)
            position = steps + (start_of(1 - half, cross_slot(d), core_) + 4 * (group % 2))
            keys(xk_op, xv_op, group, at_row, source[d, 2 * group : 2 * group + 2], position, x_tab[group])

    contract = (((1,), (1,)), ((), ()))

    def mix(q, k_ref, v_ref, group, spans, state):
        for begin, end in spans:
            span = pl.ds(begin, end - begin)
            scores = lax.dot_general(q, k_ref[group, span, :], contract, preferred_element_type=F32)
            top = jnp.broadcast_to(jnp.max(scores, axis=1, keepdims=True), (q.shape[0], 128))
            if state is not None:
                top = jnp.maximum(state[0], top)
            expo = jnp.exp(scores - jnp.concatenate([top] * ((end - begin) // 128), axis=1)).astype(BF)
            acc = jnp.dot(expo, v_ref[group, span, :], preferred_element_type=F32)
            if state is not None:
                acc += state[1] * jnp.exp(state[0] - top)
            state = (top, acc)
        return state

    outs = []

    def give(e, group):
        d = ARRIVAL[e]
        for pair in range(2):
            acc = sums[group, e * 256 + pair * 128 : e * 256 + pair * 128 + 128, :]
            position = steps + (start_of(half, slot(d), core) + 4 * pair)
            out = jnp.where(position < length, acc / pltpu.roll(acc, 64, 1), 0.0)
            attn[d, 2 * group + pair] = jnp.where(low64, pltpu.roll(out[0:64], 64, 1), out[64:128]).astype(BF)
        part = pl.ds(2 * group, 2)
        src, dst = attn.at[d, part], back.at[cls, part]
        if d > 0:
            copy = remote(src, dst, out_send.at[group, d - 1], out_recv.at[group, d - 1], device(d))
        else:
            copy = pltpu.make_async_copy(src, dst, own_sem.at[group])
        copy.start()
        outs.append(copy)

    def attend_half(group):
        for e in range(4):
            prepare(e, group)
        spans = [(begin, begin + 512) for begin in range(0, 2048, 512)]
        tops[group], sums[group] = mix(q_op[group], k_op, v_op, group, spans, None)

    def attend_cross(group):
        for e in range(4):
            prepare_cross(e, group)
        first = 128 * (group % 2)
        rows = [pl.ds(e * 256 + first, 128) for e in range(4)]
        q, top, acc = [jnp.concatenate([ref[group, r, :] for r in rows], axis=0) for ref in (q_op, tops, sums)]
        _, acc = mix(q, xk_op, xv_op, group, ((0, 512), (512, 1024)), (top, acc))
        for e in range(4):
            sums[group, rows[e], :] = acc[e * 128 : e * 128 + 128]
        for e in (3, 1, 2, 0):
            give(e, group)

    def exchange(turn):
        stay(turn)
        arrived(turn)
        if turn == 0:
            mark()
        for d in ARRIVAL[1:]:
            sort(d, turn)
            send(d, turn)
        sort(0, turn)
        share(0, turn)

    for step in range(PLACES):
        project(step)
        if step == 0:
            loads[1].wait()
            loads[2].wait()
        fill(step, 0)
        if step == 0:
            pl.semaphore_wait(barrier, DEVICES - 1)
        leave(step, 0)
    for step in range(PLACES):
        fill(step, 1)
        leave(step, 1)
    for step in range(PLACES):
        fill(step, 2)
    exchange(0)
    for step in range(PLACES):
        leave(step, 2)
    exchange(1)
    for d in ARRIVAL[1:]:
        share(d, 0)
    attend_half(0)
    exchange(2)
    for d in ARRIVAL[1:]:
        share(d, 1)
    for d in ARRIVAL:
        share_cross(d, 0)
    attend_half(1)
    for d in ARRIVAL[1:]:
        share(d, 2)
    for d in ARRIVAL:
        share_cross(d, 1)
    attend_cross(0)
    attend_half(2)
    for d in ARRIVAL:
        share_cross(d, 2)
    attend_cross(1)
    attend_cross(2)
    for copy in outs:
        copy.wait()
    for group in range(3):
        left(group)
        for d in range(4):
            if d > 0:
                sends[d, group].wait_send()
            sib_copies[d, group].wait_send()
            x_copies[d, group].wait_send()
            xs_copies[d, group].wait_send()


def layer(tiles, dest, w_in, gain, w_qkv, valid):
    hbm = pl.BlockSpec(memory_space=pltpu.HBM)
    dma = pltpu.SemaphoreType.DMA
    blocks = DEVICES // PLACES
    return pl.pallas_call(
        layer_kernel,
        out_shape=jax.ShapeDtypeStruct((4, 6, 64, 128), BF),
        in_specs=[hbm] * 5 + [pl.BlockSpec(memory_space=pltpu.SMEM)],
        out_specs=hbm,
        scratch_shapes=[
            pltpu.VMEM((PLACES, blocks, BLOCK, E), BF),
            pltpu.VMEM((E, D), BF),
            pltpu.VMEM((D, 3 * D), BF),
            pltpu.VMEM((8, 128), I32),
            pltpu.VMEM((D // 128, 128), F32),
            pltpu.VMEM((PLACES, CHUNK, D), BF),
            *[pltpu.VMEM((blocks, PLACES, BLOCK, width), BF) for width in WIDTHS],
            *[pltpu.VMEM((DEVICES, BLOCK, width), BF) for width in WIDTHS],
            pltpu.VMEM((4, 256, ROWS), BF),
            pltpu.VMEM((4, 18, 64, 128), BF),
            pltpu.VMEM((4, 12, 64, 128), BF),
            pltpu.VMEM((4, 6, 64, 128), BF),
            pltpu.VMEM((4, 6, 64, 128), BF),
            pltpu.VMEM((3, 18, 64, 128), BF),
            pltpu.VMEM((3, 1024, 128), BF),
            pltpu.VMEM((3, 2048, 128), BF),
            pltpu.VMEM((3, 2048, 128), BF),
            pltpu.VMEM((3, 1024, 128), BF),
            pltpu.VMEM((3, 1024, 128), BF),
            pltpu.VMEM((3, 1024, 128), F32),
            pltpu.VMEM((3, 1024, 128), F32),
            pltpu.VMEM((4, 6, 64, 128), BF),
            pltpu.VMEM((2, 128, 128), BF),
            pltpu.VMEM((3, 128, 128), BF),
            pltpu.VMEM((3, 128, 128), BF),
            dma((4 + PLACES,)),
            dma((3,)),
            dma((3,)),
            dma((3,)),
            dma((3, 3)),
            dma((3, 3)),
            *[dma((4, 3)) for _ in range(6)],
            dma((3, 3)),
            dma((3, 3)),
            dma((3,)),
        ],
        compiler_params=pltpu.CompilerParams(collective_id=0, has_side_effects=True, vmem_limit_bytes=VMEM_LIMIT),
        name="layer",
    )(tiles, dest, w_in, gain, w_qkv, valid)


def output_kernel(rows_hbm, weight_hbm, out, rows_in, weight, spread, packed, load_sem, out_sem):
    loads = [
        pltpu.make_async_copy(weight_hbm, weight, load_sem.at[0]),
        pltpu.make_async_copy(rows_hbm, rows_in, load_sem.at[1]),
    ]
    for copy in loads:
        copy.start()
    for copy in loads:
        copy.wait()
    low = iota((64, 128), 1) < 64
    for cls in range(4):
        heads = [weight[(cls + 4 * g) * 64 : (cls + 4 * g + 1) * 64, :] for g in range(3)]
        wide = jnp.concatenate([w for w in heads for _ in range(2)], axis=0)
        columns = []
        for g in range(3):
            tiles = [rows_in[cls, 2 * g + a // 2] for a in range(4)]
            masked = [jnp.where(low == (a % 2 == 0), tile, jnp.zeros_like(tile)) for a, tile in enumerate(tiles)]
            columns.append(jnp.concatenate(masked, axis=0))
        rows = jnp.concatenate(columns, axis=1)
        total = jnp.dot(rows, wide, preferred_element_type=F32)
        for a in range(4):
            residue = cls + (a % 2) * 8 + (a // 2) * 4
            for t in range(D // 128):
                spread[t, pl.ds(residue, 64, stride=16), :] = total[a * 64 : a * 64 + 64, t * 128 : t * 128 + 128]
    copies = []
    for index in range(4):
        span = pl.ds(index * 256, 256)
        for t in range(D // 128):
            packed[span, t * 128 : t * 128 + 128] = spread[t, span, :].astype(BF)
        copy = pltpu.make_async_copy(packed.at[span], out.at[span], out_sem.at[index])
        copy.start()
        copies.append(copy)
    for copy in copies:
        copy.wait()


def output(rows_in, weight):
    hbm = pl.BlockSpec(memory_space=pltpu.HBM)
    return pl.pallas_call(
        output_kernel,
        out_shape=jax.ShapeDtypeStruct((ROWS, D), BF),
        in_specs=[hbm, hbm],
        out_specs=hbm,
        scratch_shapes=[
            pltpu.VMEM((4, 6, 64, 128), BF),
            pltpu.VMEM((D, D), BF),
            pltpu.VMEM((D // 128, ROWS, 128), F32),
            pltpu.VMEM((ROWS, D), BF),
            pltpu.SemaphoreType.DMA((2,)),
            pltpu.SemaphoreType.DMA((4,)),
        ],
        compiler_params=pltpu.CompilerParams(vmem_limit_bytes=VMEM_LIMIT),
        name="output",
    )(rows_in, weight)


def local(tiles, destination, valid_len, in_weight, norm_gain, qkv_weight, out_weight):
    blocks = DEVICES // PLACES
    back = layer(
        tiles.reshape(blocks, PLACES, BLOCK, E),
        destination.reshape(8, 128),
        in_weight,
        norm_gain.reshape(D // 128, 128),
        qkv_weight,
        valid_len,
    )
    return output(back, out_weight).reshape(1, ROWS, D)


def solution(mesh):
    in_specs = (P(("slide", "seq"), None), P(("slide", "seq")), P(), P(), P(), P(), P())
    return jax.shard_map(local, mesh=mesh, in_specs=in_specs, out_specs=P("slide", "seq", None), check_vma=False)
```

```python
import functools

import jax
import jax.numpy as jnp
from jax import lax
from jax.experimental import pallas as pl
from jax.experimental.pallas import tpu as pltpu
from jax.sharding import PartitionSpec as P

MESH = pl.DeviceIdType.MESH
SLIDES = 8
SEQ = 16
DEVICES = 128
ROWS = 1024
BLOCK = 8
E = 1536
D = 768
PLACES = 4
CHUNK = 256
VMEM_LIMIT = 63 * 1024 * 1024
BF = jnp.bfloat16
F32 = jnp.float32
I32 = jnp.int32


def iota(shape, dim):
    return lax.broadcasted_iota(I32, shape, dim)


WIDTHS = (256, 384)
NEEDS = (((1, 0), (2, 0), (0, 0)), ((1, 1), (2, 1), (0, 1), (0, 2), (1, 2), (2, 2)))


def pick_columns(turn, columns, place):
    rows = place.shape[0]
    lane = iota((rows, 128), 1)
    cls = place & 3
    high = cls >= 2
    odd = (cls & 1) == 1
    low_lane = lane < 64
    heads = [jnp.where(high, block[:, 128:256], block[:, 0:128]) for block in columns]

    def pair(left, right):
        moved = pltpu.roll(jnp.where(odd, left, right), 64, 1)
        return jnp.where(low_lane == odd, moved, jnp.where(odd, right, left))

    picked = [pair(heads[0], heads[1])]
    if turn == 0:
        step = (place >> 2) & 3
        sorted_at = cls * 256 + (((step & 1) << 1) | (step >> 1)) * 64 + (place >> 4)
        ids = jnp.where(lane == 64, sorted_at >> 7, jnp.where(lane == 65, sorted_at & 127, 0)).astype(F32)
        q = heads[2] * 0.125
        picked.append(jnp.where(low_lane, jnp.where(odd, pltpu.roll(q, 64, 1), q), ids))
    if turn == 1:
        picked.append(pair(heads[2] * 0.125, heads[3] * 0.125))
        picked.append(pair(heads[4], heads[5]))
    return picked


ARRIVAL = (0, 2, 1, 3)
PAIR_OF = ((0, 1), (2, 3), (1, 0))
LN2 = (0.69140625, 0.0017409306)
LN3 = (1.1015625, -0.0029502113)

def key_table(group, inner):
    lane = iota((128, 128), 1)
    key = iota((128, 128), 0) // 64 + 2 * (group % 2)
    third, second = PAIR_OF[group]
    query = jnp.where(lane < 69, lane - 65, lane - 69)
    used = (lane >= 65) & (lane < 73)
    twice = used & ((query == third) | (query == second))
    thrice = used & (query == third) & (key == third)
    first = lane < 69
    ln2 = jnp.where(first, LN2[0], LN2[1])
    ln3 = jnp.where(first, LN3[0], LN3[1])
    if inner:
        return jnp.where(thrice, ln3, jnp.where(twice, ln2, 0.0))
    return jnp.where(thrice, ln2, 0.0)


def layer_kernel(
    tiles, dest, w_in, gain, w_qkv, valid, back,
    tiles_v, w_in_v, w_qkv_v, dest_v, gain_v, normed_v, out0, out1, in0, in1, hot,
    own, sib, x_own, x_sib, stage, q_op, k_op, v_op, xk_op, xv_op, tops, sums, attn, q_tab, k_tab, x_tab,
    load_sem, go_sem, come_sem, stay_sem,
    send_sem, recv_sem, sib_send, sib_recv, x_send, x_recv, xs_send, xs_recv, out_send, out_recv, own_sem,
):
    slide = lax.axis_index("slide")
    seq = lax.axis_index("seq")
    me = slide * SEQ + seq
    across = seq // PLACES
    place_me = lax.rem(seq, PLACES)
    half = seq // 8
    row = lax.rem(seq // 4, 2)
    col = lax.rem(seq // 2, 2)
    core = lax.rem(seq, 2)
    leaving, coming = (out0, out1), (in0, in1)

    def place_at(step):
        return lax.rem(place_me + step, PLACES)

    loads = [
        pltpu.make_async_copy(w_in, w_in_v, load_sem.at[0]),
        pltpu.make_async_copy(w_qkv, w_qkv_v, load_sem.at[1]),
        pltpu.make_async_copy(dest, dest_v, load_sem.at[2]),
        pltpu.make_async_copy(gain, gain_v, load_sem.at[3]),
    ]
    for step in range(PLACES):
        loads.append(pltpu.make_async_copy(tiles.at[:, place_at(step)], tiles_v.at[step], load_sem.at[4 + step]))
    for index in (0, 4, 2, 3, 1, 5, 6, 7):
        loads[index].start()

    barrier = pltpu.get_barrier_semaphore()

    @pl.loop(1, DEVICES)
    def _(i):
        other = lax.rem(me + i, DEVICES)
        pl.semaphore_signal(barrier, inc=1, device_id=(other // SEQ, lax.rem(other, SEQ)), device_id_type=MESH)

    def project(step):
        x = tiles_v[step].reshape(CHUNK, E)
        proj = jnp.dot(x, w_in_v[...], preferred_element_type=F32).astype(BF).astype(F32)
        mean = jnp.mean(proj, axis=-1, keepdims=True)
        centred = proj - mean
        var = jnp.mean(centred * centred, axis=-1, keepdims=True)
        gains = jnp.concatenate([gain_v[i : i + 1, :] for i in range(D // 128)], axis=1)
        normed_v[step] = (centred * lax.rsqrt(var + 1e-05) * gains).astype(BF)

    def fill(step, turn):
        place = place_at(step)
        normed = normed_v[step]
        columns = [
            jnp.dot(normed, w_qkv_v[:, kind * D + group * 256 : kind * D + group * 256 + 256], preferred_element_type=F32)
            for kind, group in NEEDS[turn]
        ]
        lines = (dest_v[...] & (ROWS - 1)).astype(F32)
        lines = jnp.broadcast_to(lines.reshape(8, 1, 128), (8, 32, 128)).reshape(CHUNK, 128)
        r = iota((CHUNK, 128), 0)
        wanted = ((r >> 3) & 3) * 32 + place * 8 + (r & 7)
        position = jnp.sum(jnp.where(iota((CHUNK, 128), 1) == wanted, lines, 0.0), axis=1, keepdims=True).astype(I32)
        for index, block in enumerate(pick_columns(turn, columns, position)):
            lanes = pl.ds(index * 128, 128)
            leaving[turn][:, place, :, lanes] = block.reshape(CHUNK // BLOCK, BLOCK, 128).astype(BF)

    def leave(step, turn):
        place = place_at(step)

        @pl.loop(0, CHUNK // BLOCK)
        def _(i):
            to_slide = lax.rem(slide + i, SLIDES)
            to_across = lax.rem(across + i // SLIDES, 4)

            @pl.when((to_slide != slide) | (to_across != across) | (place != place_me))
            def _():
                pltpu.make_async_remote_copy(
                    src_ref=leaving[turn].at[to_slide * 4 + to_across, place],
                    dst_ref=coming[turn].at[me],
                    send_sem=go_sem.at[turn],
                    recv_sem=come_sem.at[turn],
                    device_id=(to_slide, to_across * PLACES + place),
                    device_id_type=MESH,
                ).start()

    def stay(turn):
        copy = pltpu.make_async_copy(
            leaving[turn].at[slide * 4 + across, place_me], coming[turn].at[me], stay_sem.at[turn]
        )
        copy.start()
        copy.wait()

    others = pl.ds(0, DEVICES - 1)

    def arrived(turn):
        part = coming[turn].at[others]
        pltpu.make_async_copy(part, part, come_sem.at[turn]).wait()

    def left(turn):
        part = coming[turn].at[others]
        pltpu.make_async_copy(part, part, go_sem.at[turn]).wait()

    def slot(d):
        return 2 * lax.rem(row + d // 2, 2) + lax.rem(col + d % 2, 2)

    def cross_slot(d):
        return 2 * lax.rem(1 - row + d // 2, 2) + lax.rem(col + d % 2, 2)

    def cls_of(d):
        return 2 * lax.rem(row + d // 2 + half, 2) + lax.rem(col + d % 2, 2)

    def device(d):
        return (slide, half * 8 + slot(d) * 2 + core)

    sibling = (slide, seq + 1 - 2 * core)
    cross = (slide, (1 - half) * 8 + cross_slot(0) * 2 + core)

    low64 = iota((64, 128), 1) < 64

    def target(d):
        return own.at[0] if d == 0 else stage.at[d - 1]

    def mark():
        lane8 = iota((8, 128), 1)
        weigh = jnp.where(lane8 == 64, 128.0, jnp.where(lane8 == 65, 1.0, 0.0)).astype(BF)
        ids = in0[...].reshape(ROWS, WIDTHS[0])[:, 128:256]
        at = lax.dot_general(weigh, ids, (((1,), (1,)), ((), ())), preferred_element_type=F32)
        at = at[0:1].astype(I32)
        for d in range(4):
            hit = (at - cls_of(d) * 256) == iota((256, ROWS), 0)
            hot[d] = jnp.where(hit, 1.0, 0.0).astype(BF)

    def sort(d, turn):
        rows_in = coming[turn][...].reshape(ROWS, WIDTHS[turn])
        found = jnp.dot(hot[d], rows_in, preferred_element_type=F32)
        ref = target(d)

        def tile(a, t):
            return found[a * 64 : a * 64 + 64, t * 128 : t * 128 + 128]

        for group, at_tile in ((0, 0),) if turn == 0 else ((1, 0), (2, 2)):
            for i in range(4):
                ref[6 * group + i] = tile((2 * (group % 2) + i) % 4, at_tile).astype(BF)
        for pair in range(2):
            even, odd = tile(2 * pair, 1), tile(2 * pair + 1, 1)
            ref[6 * turn + 4 + pair] = jnp.where(low64, even, pltpu.roll(odd, 64, 1)).astype(BF)
            if turn == 1:
                ref[16 + pair] = jnp.where(low64, pltpu.roll(even, 64, 1), odd).astype(BF)

    def remote(src, dst, send, recv_, to):
        return pltpu.make_async_remote_copy(
            src_ref=src, dst_ref=dst, send_sem=send, recv_sem=recv_, device_id=to, device_id_type=MESH
        )

    sends = {}

    def send(d, group):
        part = pl.ds(6 * group, 6)
        copy = remote(
            stage.at[d - 1, part], own.at[d, part], send_sem.at[d - 1, group], recv_sem.at[d - 1, group], device(d)
        )
        copy.start()
        sends[d, group] = copy

    sib_copies, x_copies, xs_copies = {}, {}, {}

    def share(d, group):
        if d > 0:
            sends[d, group].wait_recv()
        sib_copies[d, group] = remote(
            own.at[d, pl.ds(6 * group, 4)], sib.at[d, pl.ds(4 * group, 4)], sib_send.at[d, group], sib_recv.at[d, group], sibling
        )
        sib_copies[d, group].start()
        x_copies[d, group] = remote(
            own.at[d, pl.ds(6 * group, 2)], x_own.at[d, pl.ds(2 * group, 2)], x_send.at[d, group], x_recv.at[d, group], cross
        )
        x_copies[d, group].start()

    def share_cross(d, group):
        x_copies[d, group].wait_recv()
        part = pl.ds(2 * group, 2)
        xs_copies[d, group] = remote(x_own.at[d, part], x_sib.at[d, part], xs_send.at[d, group], xs_recv.at[d, group], sibling)
        xs_copies[d, group].start()

    cls = cls_of(0)
    length = valid[slide]
    lane = iota((128, 128), 1)
    low_lane = lane < 64
    line = iota((128, 128), 0)
    steps = lax.rem(line, 64) * 16 + (line // 64) * 8

    def start_of(half_, slot_, core_):
        return half_ * 8192 + slot_ * 2048 + core_ * 1024 + cls

    for pair in range(2):
        residue = line // 64 + 2 * pair
        ones = jnp.where((lane == 64) | (lane == 65 + residue) | (lane == 69 + residue), 1.0, 0.0)
        q_tab[pair] = ones.astype(BF)
    for group in range(3):
        k_tab[group] = key_table(group, True).astype(BF)
        x_tab[group] = key_table(group, False).astype(BF)

    def keys(k_ref, v_ref, group, at_row, block, position, table):
        block = block.reshape(128, 128)
        bias = jnp.where((lane == 64) & (position >= length), jnp.full_like(block, -1e30), table)
        k_ref[group, at_row : at_row + 128, :] = jnp.where(low_lane, block, bias)
        v_ref[group, at_row : at_row + 128, :] = jnp.where(low_lane, jnp.ones_like(block), block)

    def prepare(e, group):
        d = ARRIVAL[e]
        for pair in range(2):
            packed = own[d, 6 * group + 4 + pair].astype(F32)
            q = jnp.concatenate([packed, pltpu.roll(packed, 64, 1)], axis=0).astype(BF)
            begin = e * 256 + pair * 128
            q_op[group, begin : begin + 128, :] = jnp.where(low_lane, q, q_tab[pair])
        sib_copies[d, group].wait_recv()
        for source, core_, first in ((own, core, 6 * group), (sib, 1 - core, 4 * group)):
            for rest in range(2):
                at_row = e * 512 + rest * 256 + (0 if source is own else 128)
                position = steps + (start_of(half, slot(d), core_) + 4 * ((group + rest) % 2))
                table = k_tab[group] if rest == 0 else jnp.zeros((128, 128), BF)
                at_tile = first + 2 * rest
                keys(k_op, v_op, group, at_row, source[d, at_tile : at_tile + 2], position, table)

    def prepare_cross(e, group):
        d = ARRIVAL[e]
        xs_copies[d, group].wait_recv()
        for source, core_ in ((x_own, core), (x_sib, 1 - core)):
            at_row = e * 256 + (0 if source is x_own else 128)
            position = steps + (start_of(1 - half, cross_slot(d), core_) + 4 * (group % 2))
            keys(xk_op, xv_op, group, at_row, source[d, 2 * group : 2 * group + 2], position, x_tab[group])

    contract = (((1,), (1,)), ((), ()))

    def mix(q, k_ref, v_ref, group, spans, state):
        for begin, end in spans:
            span = pl.ds(begin, end - begin)
            scores = lax.dot_general(q, k_ref[group, span, :], contract, preferred_element_type=F32)
            top = jnp.broadcast_to(jnp.max(scores, axis=1, keepdims=True), (q.shape[0], 128))
            if state is not None:
                top = jnp.maximum(state[0], top)
            expo = jnp.exp(scores - jnp.concatenate([top] * ((end - begin) // 128), axis=1)).astype(BF)
            acc = jnp.dot(expo, v_ref[group, span, :], preferred_element_type=F32)
            if state is not None:
                acc += state[1] * jnp.exp(state[0] - top)
            state = (top, acc)
        return state

    outs = []

    def give(e, group):
        d = ARRIVAL[e]
        for pair in range(2):
            acc = sums[group, e * 256 + pair * 128 : e * 256 + pair * 128 + 128, :]
            position = steps + (start_of(half, slot(d), core) + 4 * pair)
            out = jnp.where(position < length, acc / pltpu.roll(acc, 64, 1), 0.0)
            attn[d, 2 * group + pair] = jnp.where(low64, pltpu.roll(out[0:64], 64, 1), out[64:128]).astype(BF)
        part = pl.ds(2 * group, 2)
        src, dst = attn.at[d, part], back.at[cls, part]
        if d > 0:
            copy = remote(src, dst, out_send.at[group, d - 1], out_recv.at[group, d - 1], device(d))
        else:
            copy = pltpu.make_async_copy(src, dst, own_sem.at[group])
        copy.start()
        outs.append(copy)

    def attend_half(group):
        for e in range(4):
            prepare(e, group)
        spans = [(begin, begin + 512) for begin in range(0, 2048, 512)]
        tops[group], sums[group] = mix(q_op[group], k_op, v_op, group, spans, None)

    def attend_cross(group):
        for e in range(4):
            prepare_cross(e, group)
        first = 128 * (group % 2)
        rows = [pl.ds(e * 256 + first, 128) for e in range(4)]
        q, top, acc = [jnp.concatenate([ref[group, r, :] for r in rows], axis=0) for ref in (q_op, tops, sums)]
        _, acc = mix(q, xk_op, xv_op, group, ((0, 512), (512, 1024)), (top, acc))
        for e in range(4):
            sums[group, rows[e], :] = acc[e * 128 : e * 128 + 128]
        for e in (3, 1, 2, 0):
            give(e, group)

    def exchange(turn):
        stay(turn)
        arrived(turn)
        if turn == 0:
            mark()
        for d in ARRIVAL[1:]:
            sort(d, turn)
            send(d, turn)
        if turn == 1:
            for d in ARRIVAL[1:]:
                send(d, 2)
        sort(0, turn)
        for group in (0,) if turn == 0 else (1, 2):
            share(0, group)

    for index in (0, 3, 4):
        loads[index].wait()
    project(0)
    for index in (1, 2):
        loads[index].wait()
    for step in range(PLACES):
        if step + 1 < PLACES:
            loads[5 + step].wait()
            project(step + 1)
        fill(step, 0)
        if step == 0:
            pl.semaphore_wait(barrier, DEVICES - 1)
        leave(step, 0)
    for step in range(PLACES):
        fill(step, 1)
        leave(step, 1)
    exchange(0)
    exchange(1)
    for d in ARRIVAL[1:]:
        share(d, 0)
    attend_half(0)
    for d in ARRIVAL[1:]:
        share(d, 1)
    for d in ARRIVAL:
        share_cross(d, 0)
    attend_half(1)
    for d in ARRIVAL[1:]:
        share(d, 2)
    for d in ARRIVAL:
        share_cross(d, 1)
    attend_cross(0)
    attend_cross(1)
    for d in ARRIVAL:
        share_cross(d, 2)
    attend_half(2)
    attend_cross(2)
    for copy in outs:
        copy.wait()
    for turn in range(2):
        left(turn)
    for group in range(3):
        for d in range(4):
            if d > 0:
                sends[d, group].wait_send()
            sib_copies[d, group].wait_send()
            x_copies[d, group].wait_send()
            xs_copies[d, group].wait_send()


def layer(tiles, dest, w_in, gain, w_qkv, valid):
    hbm = pl.BlockSpec(memory_space=pltpu.HBM)
    dma = pltpu.SemaphoreType.DMA
    blocks = DEVICES // PLACES
    return pl.pallas_call(
        layer_kernel,
        out_shape=jax.ShapeDtypeStruct((4, 6, 64, 128), BF),
        in_specs=[hbm] * 5 + [pl.BlockSpec(memory_space=pltpu.SMEM)],
        out_specs=hbm,
        scratch_shapes=[
            pltpu.VMEM((PLACES, blocks, BLOCK, E), BF),
            pltpu.VMEM((E, D), BF),
            pltpu.VMEM((D, 3 * D), BF),
            pltpu.VMEM((8, 128), I32),
            pltpu.VMEM((D // 128, 128), F32),
            pltpu.VMEM((PLACES, CHUNK, D), BF),
            *[pltpu.VMEM((blocks, PLACES, BLOCK, width), BF) for width in WIDTHS],
            *[pltpu.VMEM((DEVICES, BLOCK, width), BF) for width in WIDTHS],
            pltpu.VMEM((4, 256, ROWS), BF),
            pltpu.VMEM((4, 18, 64, 128), BF),
            pltpu.VMEM((4, 12, 64, 128), BF),
            pltpu.VMEM((4, 6, 64, 128), BF),
            pltpu.VMEM((4, 6, 64, 128), BF),
            pltpu.VMEM((3, 18, 64, 128), BF),
            pltpu.VMEM((3, 1024, 128), BF),
            pltpu.VMEM((3, 2048, 128), BF),
            pltpu.VMEM((3, 2048, 128), BF),
            pltpu.VMEM((3, 1024, 128), BF),
            pltpu.VMEM((3, 1024, 128), BF),
            pltpu.VMEM((3, 1024, 128), F32),
            pltpu.VMEM((3, 1024, 128), F32),
            pltpu.VMEM((4, 6, 64, 128), BF),
            pltpu.VMEM((2, 128, 128), BF),
            pltpu.VMEM((3, 128, 128), BF),
            pltpu.VMEM((3, 128, 128), BF),
            dma((4 + PLACES,)),
            dma((3,)),
            dma((3,)),
            dma((3,)),
            dma((3, 3)),
            dma((3, 3)),
            *[dma((4, 3)) for _ in range(6)],
            dma((3, 3)),
            dma((3, 3)),
            dma((3,)),
        ],
        compiler_params=pltpu.CompilerParams(collective_id=0, has_side_effects=True, vmem_limit_bytes=VMEM_LIMIT),
        name="layer",
    )(tiles, dest, w_in, gain, w_qkv, valid)


def output_kernel(rows_hbm, weight_hbm, out, rows_in, weight, spread, packed, load_sem, out_sem):
    loads = [
        pltpu.make_async_copy(weight_hbm, weight, load_sem.at[0]),
        pltpu.make_async_copy(rows_hbm, rows_in, load_sem.at[1]),
    ]
    for copy in loads:
        copy.start()
    for copy in loads:
        copy.wait()
    low = iota((64, 128), 1) < 64
    for cls in range(4):
        heads = [weight[(cls + 4 * g) * 64 : (cls + 4 * g + 1) * 64, :] for g in range(3)]
        wide = jnp.concatenate([w for w in heads for _ in range(2)], axis=0)
        columns = []
        for g in range(3):
            tiles = [rows_in[cls, 2 * g + a // 2] for a in range(4)]
            masked = [jnp.where(low == (a % 2 == 0), tile, jnp.zeros_like(tile)) for a, tile in enumerate(tiles)]
            columns.append(jnp.concatenate(masked, axis=0))
        rows = jnp.concatenate(columns, axis=1)
        total = jnp.dot(rows, wide, preferred_element_type=F32)
        for a in range(4):
            residue = cls + (a % 2) * 8 + (a // 2) * 4
            for t in range(D // 128):
                spread[t, pl.ds(residue, 64, stride=16), :] = total[a * 64 : a * 64 + 64, t * 128 : t * 128 + 128]
    copies = []
    for index in range(4):
        span = pl.ds(index * 256, 256)
        for t in range(D // 128):
            packed[span, t * 128 : t * 128 + 128] = spread[t, span, :].astype(BF)
        copy = pltpu.make_async_copy(packed.at[span], out.at[span], out_sem.at[index])
        copy.start()
        copies.append(copy)
    for copy in copies:
        copy.wait()


def output(rows_in, weight):
    hbm = pl.BlockSpec(memory_space=pltpu.HBM)
    return pl.pallas_call(
        output_kernel,
        out_shape=jax.ShapeDtypeStruct((ROWS, D), BF),
        in_specs=[hbm, hbm],
        out_specs=hbm,
        scratch_shapes=[
            pltpu.VMEM((4, 6, 64, 128), BF),
            pltpu.VMEM((D, D), BF),
            pltpu.VMEM((D // 128, ROWS, 128), F32),
            pltpu.VMEM((ROWS, D), BF),
            pltpu.SemaphoreType.DMA((2,)),
            pltpu.SemaphoreType.DMA((4,)),
        ],
        compiler_params=pltpu.CompilerParams(vmem_limit_bytes=VMEM_LIMIT),
        name="output",
    )(rows_in, weight)


def local(tiles, destination, valid_len, in_weight, norm_gain, qkv_weight, out_weight):
    blocks = DEVICES // PLACES
    back = layer(
        tiles.reshape(blocks, PLACES, BLOCK, E),
        destination.reshape(8, 128),
        in_weight,
        norm_gain.reshape(D // 128, 128),
        qkv_weight,
        valid_len,
    )
    return output(back, out_weight).reshape(1, ROWS, D)


def solution(mesh):
    in_specs = (P(("slide", "seq"), None), P(("slide", "seq")), P(), P(), P(), P(), P())
    return jax.shard_map(local, mesh=mesh, in_specs=in_specs, out_specs=P("slide", "seq", None), check_vma=False)
```

```python
import functools

import jax
import jax.numpy as jnp
from jax import lax
from jax.experimental import pallas as pl
from jax.experimental.pallas import tpu as pltpu
from jax.sharding import PartitionSpec as P

MESH = pl.DeviceIdType.MESH
SLIDES = 8
SEQ = 16
DEVICES = 128
ROWS = 1024
BLOCK = 8
E = 1536
D = 768
PLACES = 4
CHUNK = 256
VMEM_LIMIT = 63 * 1024 * 1024
BF = jnp.bfloat16
F32 = jnp.float32
I32 = jnp.int32


def iota(shape, dim):
    return lax.broadcasted_iota(I32, shape, dim)


WIDTHS = (256, 384)
NEEDS = (((1, 0), (2, 0), (0, 0)), ((1, 1), (2, 1), (0, 1), (0, 2), (1, 2), (2, 2)))


def pick_columns(turn, columns, place):
    rows = place.shape[0]
    lane = iota((rows, 128), 1)
    cls = place & 3
    high = cls >= 2
    odd = (cls & 1) == 1
    low_lane = lane < 64
    heads = [jnp.where(high, block[:, 128:256], block[:, 0:128]) for block in columns]

    def pair(left, right):
        moved = pltpu.roll(jnp.where(odd, left, right), 64, 1)
        return jnp.where(low_lane == odd, moved, jnp.where(odd, right, left))

    picked = [pair(heads[0], heads[1])]
    if turn == 0:
        step = (place >> 2) & 3
        sorted_at = cls * 256 + (((step & 1) << 1) | (step >> 1)) * 64 + (place >> 4)
        ids = jnp.where(lane == 64, sorted_at >> 7, jnp.where(lane == 65, sorted_at & 127, 0)).astype(F32)
        q = heads[2] * 0.125
        picked.append(jnp.where(low_lane, jnp.where(odd, pltpu.roll(q, 64, 1), q), ids))
    if turn == 1:
        picked.append(pair(heads[2] * 0.125, heads[3] * 0.125))
        picked.append(pair(heads[4], heads[5]))
    return picked


ARRIVAL = (0, 2, 1, 3)
PAIR_OF = ((0, 1), (2, 3), (1, 0))
LN2 = (0.69140625, 0.0017409306)
LN3 = (1.1015625, -0.0029502113)

def key_table(group, inner):
    lane = iota((128, 128), 1)
    key = iota((128, 128), 0) // 64 + 2 * (group % 2)
    third, second = PAIR_OF[group]
    query = jnp.where(lane < 69, lane - 65, lane - 69)
    used = (lane >= 65) & (lane < 73)
    twice = used & ((query == third) | (query == second))
    thrice = used & (query == third) & (key == third)
    first = lane < 69
    ln2 = jnp.where(first, LN2[0], LN2[1])
    ln3 = jnp.where(first, LN3[0], LN3[1])
    if inner:
        return jnp.where(thrice, ln3, jnp.where(twice, ln2, 0.0))
    return jnp.where(thrice, ln2, 0.0)


def layer_kernel(
    tiles, dest, w_in, gain, w_qkv, valid, back,
    tiles_v, w_in_v, w_qkv_v, dest_v, gain_v, normed_v, out0, out1, in0, in1, hot,
    own, sib, x_own, x_sib, stage, q_op, k_op, v_op, xk_op, xv_op, tops, sums, attn, q_tab, k_tab, x_tab,
    load_sem, go_sem, come_sem, stay_sem,
    send_sem, recv_sem, sib_send, sib_recv, x_send, x_recv, xs_send, xs_recv, out_send, out_recv, own_sem,
):
    slide = lax.axis_index("slide")
    seq = lax.axis_index("seq")
    me = slide * SEQ + seq
    across = seq // PLACES
    place_me = lax.rem(seq, PLACES)
    half = seq // 8
    row = lax.rem(seq // 4, 2)
    col = lax.rem(seq // 2, 2)
    core = lax.rem(seq, 2)
    leaving, coming = (out0, out1), (in0, in1)

    def place_at(step):
        return lax.rem(place_me + step, PLACES)

    loads = [
        pltpu.make_async_copy(w_in, w_in_v, load_sem.at[0]),
        pltpu.make_async_copy(w_qkv, w_qkv_v, load_sem.at[1]),
        pltpu.make_async_copy(dest, dest_v, load_sem.at[2]),
        pltpu.make_async_copy(gain, gain_v, load_sem.at[3]),
    ]
    for step in range(PLACES):
        loads.append(pltpu.make_async_copy(tiles.at[:, place_at(step)], tiles_v.at[step], load_sem.at[4 + step]))
    for index in (0, 4, 2, 3, 1, 5, 6, 7):
        loads[index].start()

    barrier = pltpu.get_barrier_semaphore()

    @pl.loop(1, DEVICES)
    def _(i):
        other = lax.rem(me + i, DEVICES)
        pl.semaphore_signal(barrier, inc=1, device_id=(other // SEQ, lax.rem(other, SEQ)), device_id_type=MESH)

    def project(step):
        x = tiles_v[step].reshape(CHUNK, E)
        proj = jnp.dot(x, w_in_v[...], preferred_element_type=F32).astype(BF).astype(F32)
        mean = jnp.mean(proj, axis=-1, keepdims=True)
        centred = proj - mean
        var = jnp.mean(centred * centred, axis=-1, keepdims=True)
        gains = jnp.concatenate([gain_v[i : i + 1, :] for i in range(D // 128)], axis=1)
        normed_v[step] = (centred * lax.rsqrt(var + 1e-05) * gains).astype(BF)

    def fill(step, turn):
        place = place_at(step)
        normed = normed_v[step]
        columns = [
            jnp.dot(normed, w_qkv_v[:, kind * D + group * 256 : kind * D + group * 256 + 256], preferred_element_type=F32)
            for kind, group in NEEDS[turn]
        ]
        lines = (dest_v[...] & (ROWS - 1)).astype(F32)
        lines = jnp.broadcast_to(lines.reshape(8, 1, 128), (8, 32, 128)).reshape(CHUNK, 128)
        r = iota((CHUNK, 128), 0)
        wanted = ((r >> 3) & 3) * 32 + place * 8 + (r & 7)
        position = jnp.sum(jnp.where(iota((CHUNK, 128), 1) == wanted, lines, 0.0), axis=1, keepdims=True).astype(I32)
        for index, block in enumerate(pick_columns(turn, columns, position)):
            lanes = pl.ds(index * 128, 128)
            leaving[turn][:, place, :, lanes] = block.reshape(CHUNK // BLOCK, BLOCK, 128).astype(BF)

    def leave(step, turn):
        place = place_at(step)

        @pl.loop(1 if step == 0 else 0, CHUNK // BLOCK)
        def _(i):
            to_slide = lax.rem(slide + i, SLIDES)
            to_across = lax.rem(across + i // SLIDES, 4)
            pltpu.make_async_remote_copy(
                src_ref=leaving[turn].at[to_slide * 4 + to_across, place],
                dst_ref=coming[turn].at[me],
                send_sem=go_sem.at[turn],
                recv_sem=come_sem.at[turn],
                device_id=(to_slide, to_across * PLACES + place),
                device_id_type=MESH,
            ).start()

    def stay(turn):
        copy = pltpu.make_async_copy(
            leaving[turn].at[slide * 4 + across, place_me], coming[turn].at[me], stay_sem.at[turn]
        )
        copy.start()
        copy.wait()

    others = pl.ds(0, DEVICES - 1)

    def arrived(turn):
        part = coming[turn].at[others]
        pltpu.make_async_copy(part, part, come_sem.at[turn]).wait()

    def left(turn):
        part = coming[turn].at[others]
        pltpu.make_async_copy(part, part, go_sem.at[turn]).wait()

    def slot(d):
        return 2 * lax.rem(row + d // 2, 2) + lax.rem(col + d % 2, 2)

    def cross_slot(d):
        return 2 * lax.rem(1 - row + d // 2, 2) + lax.rem(col + d % 2, 2)

    def cls_of(d):
        return 2 * lax.rem(row + d // 2 + half, 2) + lax.rem(col + d % 2, 2)

    def device(d):
        return (slide, half * 8 + slot(d) * 2 + core)

    sibling = (slide, seq + 1 - 2 * core)
    cross = (slide, (1 - half) * 8 + cross_slot(0) * 2 + core)

    low64 = iota((64, 128), 1) < 64

    def target(d):
        return own.at[0] if d == 0 else stage.at[d - 1]

    def mark():
        lane8 = iota((8, 128), 1)
        weigh = jnp.where(lane8 == 64, 128.0, jnp.where(lane8 == 65, 1.0, 0.0)).astype(BF)
        ids = in0[...].reshape(ROWS, WIDTHS[0])[:, 128:256]
        at = lax.dot_general(weigh, ids, (((1,), (1,)), ((), ())), preferred_element_type=F32)
        at = at[0:1].astype(I32)
        for d in range(4):
            hit = (at - cls_of(d) * 256) == iota((256, ROWS), 0)
            hot[d] = jnp.where(hit, 1.0, 0.0).astype(BF)

    def sort(d, turn):
        rows_in = coming[turn][...].reshape(ROWS, WIDTHS[turn])
        found = jnp.dot(hot[d], rows_in, preferred_element_type=F32)
        ref = target(d)

        def tile(a, t):
            return found[a * 64 : a * 64 + 64, t * 128 : t * 128 + 128]

        for group, at_tile in ((0, 0),) if turn == 0 else ((1, 0), (2, 2)):
            for i in range(4):
                ref[6 * group + i] = tile((2 * (group % 2) + i) % 4, at_tile).astype(BF)
        for pair in range(2):
            even, odd = tile(2 * pair, 1), tile(2 * pair + 1, 1)
            ref[6 * turn + 4 + pair] = jnp.where(low64, even, pltpu.roll(odd, 64, 1)).astype(BF)
            if turn == 1:
                ref[16 + pair] = jnp.where(low64, pltpu.roll(even, 64, 1), odd).astype(BF)

    def remote(src, dst, send, recv_, to):
        return pltpu.make_async_remote_copy(
            src_ref=src, dst_ref=dst, send_sem=send, recv_sem=recv_, device_id=to, device_id_type=MESH
        )

    sends = {}

    def send(d, group):
        part = pl.ds(6 * group, 6)
        copy = remote(
            stage.at[d - 1, part], own.at[d, part], send_sem.at[d - 1, group], recv_sem.at[d - 1, group], device(d)
        )
        copy.start()
        sends[d, group] = copy

    sib_copies, x_copies, xs_copies = {}, {}, {}

    def share(d, group):
        if d > 0:
            sends[d, group].wait_recv()
        sib_copies[d, group] = remote(
            own.at[d, pl.ds(6 * group, 4)], sib.at[d, pl.ds(4 * group, 4)], sib_send.at[d, group], sib_recv.at[d, group], sibling
        )
        sib_copies[d, group].start()
        x_copies[d, group] = remote(
            own.at[d, pl.ds(6 * group, 2)], x_own.at[d, pl.ds(2 * group, 2)], x_send.at[d, group], x_recv.at[d, group], cross
        )
        x_copies[d, group].start()

    def share_cross(d, group):
        x_copies[d, group].wait_recv()
        part = pl.ds(2 * group, 2)
        xs_copies[d, group] = remote(x_own.at[d, part], x_sib.at[d, part], xs_send.at[d, group], xs_recv.at[d, group], sibling)
        xs_copies[d, group].start()

    cls = cls_of(0)
    length = valid[slide]
    lane = iota((128, 128), 1)
    low_lane = lane < 64
    line = iota((128, 128), 0)
    steps = lax.rem(line, 64) * 16 + (line // 64) * 8

    def start_of(half_, slot_, core_):
        return half_ * 8192 + slot_ * 2048 + core_ * 1024 + cls

    for pair in range(2):
        residue = line // 64 + 2 * pair
        ones = jnp.where((lane == 64) | (lane == 65 + residue) | (lane == 69 + residue), 1.0, 0.0)
        q_tab[pair] = ones.astype(BF)
    for group in range(3):
        k_tab[group] = key_table(group, True).astype(BF)
        x_tab[group] = key_table(group, False).astype(BF)

    def keys(k_ref, v_ref, group, at_row, block, position, table):
        block = block.reshape(128, 128)
        bias = jnp.where((lane == 64) & (position >= length), jnp.full_like(block, -1e30), table)
        k_ref[group, at_row : at_row + 128, :] = jnp.where(low_lane, block, bias)
        v_ref[group, at_row : at_row + 128, :] = jnp.where(low_lane, jnp.ones_like(block), block)

    def prepare(e, group):
        d = ARRIVAL[e]
        for pair in range(2):
            packed = own[d, 6 * group + 4 + pair].astype(F32)
            q = jnp.concatenate([packed, pltpu.roll(packed, 64, 1)], axis=0).astype(BF)
            begin = e * 256 + pair * 128
            q_op[group, begin : begin + 128, :] = jnp.where(low_lane, q, q_tab[pair])
        sib_copies[d, group].wait_recv()
        for source, core_, first in ((own, core, 6 * group), (sib, 1 - core, 4 * group)):
            for rest in range(2):
                at_row = e * 512 + rest * 256 + (0 if source is own else 128)
                position = steps + (start_of(half, slot(d), core_) + 4 * ((group + rest) % 2))
                table = k_tab[group] if rest == 0 else jnp.zeros((128, 128), BF)
                at_tile = first + 2 * rest
                keys(k_op, v_op, group, at_row, source[d, at_tile : at_tile + 2], position, table)

    def prepare_cross(e, group):
        d = ARRIVAL[e]
        xs_copies[d, group].wait_recv()
        for source, core_ in ((x_own, core), (x_sib, 1 - core)):
            at_row = e * 256 + (0 if source is x_own else 128)
            position = steps + (start_of(1 - half, cross_slot(d), core_) + 4 * (group % 2))
            keys(xk_op, xv_op, group, at_row, source[d, 2 * group : 2 * group + 2], position, x_tab[group])

    contract = (((1,), (1,)), ((), ()))

    def mix(q, k_ref, v_ref, group, spans, state):
        for begin, end in spans:
            span = pl.ds(begin, end - begin)
            scores = lax.dot_general(q, k_ref[group, span, :], contract, preferred_element_type=F32)
            top = jnp.broadcast_to(jnp.max(scores, axis=1, keepdims=True), (q.shape[0], 128))
            if state is not None:
                top = jnp.maximum(state[0], top)
            expo = jnp.exp(scores - jnp.concatenate([top] * ((end - begin) // 128), axis=1)).astype(BF)
            acc = jnp.dot(expo, v_ref[group, span, :], preferred_element_type=F32)
            if state is not None:
                acc += state[1] * jnp.exp(state[0] - top)
            state = (top, acc)
        return state

    outs = []

    def give(e, group, pair):
        d = ARRIVAL[e]
        acc = sums[group, e * 256 + pair * 128 : e * 256 + pair * 128 + 128, :]
        position = steps + (start_of(half, slot(d), core) + 4 * pair)
        out = jnp.where(position < length, acc / pltpu.roll(acc, 64, 1), 0.0)
        attn[d, 2 * group + pair] = jnp.where(low64, pltpu.roll(out[0:64], 64, 1), out[64:128]).astype(BF)
        src, dst = attn.at[d, 2 * group + pair], back.at[cls, 2 * group + pair]
        if d > 0:
            copy = remote(src, dst, out_send.at[2 * group + pair, d - 1], out_recv.at[2 * group + pair, d - 1], device(d))
        else:
            copy = pltpu.make_async_copy(src, dst, own_sem.at[2 * group + pair])
        copy.start()
        outs.append(copy)

    def attend_half(group):
        for e in range(4):
            prepare(e, group)
        spans = [(begin, begin + 512) for begin in range(0, 2048, 512)]
        tops[group], sums[group] = mix(q_op[group], k_op, v_op, group, spans, None)
        for e in (3, 1, 2, 0):
            give(e, group, 1 - group % 2)

    def attend_cross(groups):
        found = []
        for group in groups:
            first = 128 * (group % 2)
            rows = [pl.ds(e * 256 + first, 128) for e in range(4)]
            q, top, acc = [jnp.concatenate([ref[group, r, :] for r in rows], axis=0) for ref in (q_op, tops, sums)]
            found.append((group, rows, mix(q, xk_op, xv_op, group, ((0, 512), (512, 1024)), (top, acc))[1]))
        for group, rows, acc in found:
            for e in range(4):
                sums[group, rows[e], :] = acc[e * 128 : e * 128 + 128]
        for group in groups:
            for e in (3, 1, 2, 0):
                give(e, group, group % 2)

    def exchange(turn):
        stay(turn)
        arrived(turn)
        if turn == 0:
            mark()
        for d in ARRIVAL[1:]:
            sort(d, turn)
            send(d, turn)
        if turn == 1:
            for d in ARRIVAL[1:]:
                send(d, 2)
        sort(0, turn)
        for group in (0,) if turn == 0 else (1, 2):
            share(0, group)

    for index in (0, 3, 4):
        loads[index].wait()
    project(0)
    for index in (1, 2):
        loads[index].wait()
    for step in range(PLACES):
        if step + 1 < PLACES:
            loads[5 + step].wait()
            project(step + 1)
        fill(step, 0)
        if step == 0:
            pl.semaphore_wait(barrier, DEVICES - 1)
        leave(step, 0)
    for step in range(PLACES):
        fill(step, 1)
        leave(step, 1)
    exchange(0)
    exchange(1)
    for d in ARRIVAL[1:]:
        share(d, 0)
    attend_half(0)
    for d in ARRIVAL[1:]:
        share(d, 1)
    for d in ARRIVAL:
        share_cross(d, 0)
    attend_half(1)
    for d in ARRIVAL[1:]:
        share(d, 2)
    for d in ARRIVAL:
        share_cross(d, 1)
    for group in range(2):
        for e in range(4):
            prepare_cross(e, group)
    attend_cross((0, 1))
    for d in ARRIVAL:
        share_cross(d, 2)
    attend_half(2)
    for e in range(4):
        prepare_cross(e, 2)
    attend_cross((2,))
    for copy in outs:
        copy.wait()
    for turn in range(2):
        left(turn)
    for group in range(3):
        for d in range(4):
            if d > 0:
                sends[d, group].wait_send()
            sib_copies[d, group].wait_send()
            x_copies[d, group].wait_send()
            xs_copies[d, group].wait_send()


def layer(tiles, dest, w_in, gain, w_qkv, valid):
    hbm = pl.BlockSpec(memory_space=pltpu.HBM)
    dma = pltpu.SemaphoreType.DMA
    blocks = DEVICES // PLACES
    return pl.pallas_call(
        layer_kernel,
        out_shape=jax.ShapeDtypeStruct((4, 6, 64, 128), BF),
        in_specs=[hbm] * 5 + [pl.BlockSpec(memory_space=pltpu.SMEM)],
        out_specs=hbm,
        scratch_shapes=[
            pltpu.VMEM((PLACES, blocks, BLOCK, E), BF),
            pltpu.VMEM((E, D), BF),
            pltpu.VMEM((D, 3 * D), BF),
            pltpu.VMEM((8, 128), I32),
            pltpu.VMEM((D // 128, 128), F32),
            pltpu.VMEM((PLACES, CHUNK, D), BF),
            *[pltpu.VMEM((blocks, PLACES, BLOCK, width), BF) for width in WIDTHS],
            *[pltpu.VMEM((DEVICES, BLOCK, width), BF) for width in WIDTHS],
            pltpu.VMEM((4, 256, ROWS), BF),
            pltpu.VMEM((4, 18, 64, 128), BF),
            pltpu.VMEM((4, 12, 64, 128), BF),
            pltpu.VMEM((4, 6, 64, 128), BF),
            pltpu.VMEM((4, 6, 64, 128), BF),
            pltpu.VMEM((3, 18, 64, 128), BF),
            pltpu.VMEM((3, 1024, 128), BF),
            pltpu.VMEM((3, 2048, 128), BF),
            pltpu.VMEM((3, 2048, 128), BF),
            pltpu.VMEM((3, 1024, 128), BF),
            pltpu.VMEM((3, 1024, 128), BF),
            pltpu.VMEM((3, 1024, 128), F32),
            pltpu.VMEM((3, 1024, 128), F32),
            pltpu.VMEM((4, 6, 64, 128), BF),
            pltpu.VMEM((2, 128, 128), BF),
            pltpu.VMEM((3, 128, 128), BF),
            pltpu.VMEM((3, 128, 128), BF),
            dma((4 + PLACES,)),
            dma((3,)),
            dma((3,)),
            dma((3,)),
            dma((3, 3)),
            dma((3, 3)),
            *[dma((4, 3)) for _ in range(6)],
            dma((6, 3)),
            dma((6, 3)),
            dma((6,)),
        ],
        compiler_params=pltpu.CompilerParams(collective_id=0, has_side_effects=True, vmem_limit_bytes=VMEM_LIMIT),
        name="layer",
    )(tiles, dest, w_in, gain, w_qkv, valid)


def output_kernel(rows_hbm, weight_hbm, out, rows_in, weight, spread, packed, load_sem, out_sem):
    loads = [pltpu.make_async_copy(rows_hbm, rows_in, load_sem.at[0])]
    for part in range(2):
        lanes = pl.ds(part * (D // 2), D // 2)
        loads.append(pltpu.make_async_copy(weight_hbm.at[:, lanes], weight.at[part], load_sem.at[1 + part]))
    for copy in loads:
        copy.start()
    loads[0].wait()
    low = iota((64, 128), 1) < 64
    rows = []
    for cls in range(4):
        columns = []
        for g in range(3):
            tiles = [rows_in[cls, 2 * g + a // 2] for a in range(4)]
            masked = [jnp.where(low == (a % 2 == 0), tile, jnp.zeros_like(tile)) for a, tile in enumerate(tiles)]
            columns.append(jnp.concatenate(masked, axis=0))
        rows.append(jnp.concatenate(columns, axis=1))
    copies = []
    for part in range(2):
        loads[1 + part].wait()
        for cls in range(4):
            heads = [weight[part, (cls + 4 * g) * 64 : (cls + 4 * g + 1) * 64, :] for g in range(3)]
            wide = jnp.concatenate([w for w in heads for _ in range(2)], axis=0)
            total = jnp.dot(rows[cls], wide, preferred_element_type=F32)
            for a in range(4):
                residue = cls + (a % 2) * 8 + (a // 2) * 4
                for t in range(3):
                    spread[3 * part + t, pl.ds(residue, 64, stride=16), :] = total[a * 64 : a * 64 + 64, t * 128 : t * 128 + 128]
        for t in range(3):
            packed[part, :, t * 128 : t * 128 + 128] = spread[3 * part + t].astype(BF)
        copy = pltpu.make_async_copy(packed.at[part], out.at[:, pl.ds(part * (D // 2), D // 2)], out_sem.at[part])
        copy.start()
        copies.append(copy)
    for copy in copies:
        copy.wait()


def output(rows_in, weight):
    hbm = pl.BlockSpec(memory_space=pltpu.HBM)
    return pl.pallas_call(
        output_kernel,
        out_shape=jax.ShapeDtypeStruct((ROWS, D), BF),
        in_specs=[hbm, hbm],
        out_specs=hbm,
        scratch_shapes=[
            pltpu.VMEM((4, 6, 64, 128), BF),
            pltpu.VMEM((2, D, D // 2), BF),
            pltpu.VMEM((D // 128, ROWS, 128), F32),
            pltpu.VMEM((2, ROWS, D // 2), BF),
            pltpu.SemaphoreType.DMA((3,)),
            pltpu.SemaphoreType.DMA((2,)),
        ],
        compiler_params=pltpu.CompilerParams(vmem_limit_bytes=VMEM_LIMIT),
        name="output",
    )(rows_in, weight)


def local(tiles, destination, valid_len, in_weight, norm_gain, qkv_weight, out_weight):
    blocks = DEVICES // PLACES
    back = layer(
        tiles.reshape(blocks, PLACES, BLOCK, E),
        destination.reshape(8, 128),
        in_weight,
        norm_gain.reshape(D // 128, 128),
        qkv_weight,
        valid_len,
    )
    return output(back, out_weight).reshape(1, ROWS, D)


def solution(mesh):
    in_specs = (P(("slide", "seq"), None), P(("slide", "seq")), P(), P(), P(), P(), P())
    return jax.shard_map(local, mesh=mesh, in_specs=in_specs, out_specs=P("slide", "seq", None), check_vma=False)
```

```python
import functools

import jax
import jax.numpy as jnp
from jax import lax
from jax.experimental import pallas as pl
from jax.experimental.pallas import tpu as pltpu
from jax.sharding import PartitionSpec as P

MESH = pl.DeviceIdType.MESH
SLIDES = 8
SEQ = 16
DEVICES = 128
ROWS = 1024
BLOCK = 8
E = 1536
D = 768
PLACES = 4
CHUNK = 256
VMEM_LIMIT = 63 * 1024 * 1024
BF = jnp.bfloat16
F32 = jnp.float32
I32 = jnp.int32


def iota(shape, dim):
    return lax.broadcasted_iota(I32, shape, dim)


WIDTHS = (256, 384)
NEEDS = (((1, 0), (2, 0), (0, 0)), ((1, 1), (2, 1), (0, 1), (0, 2), (1, 2), (2, 2)))


def pick_columns(turn, columns, place):
    rows = place.shape[0]
    lane = iota((rows, 128), 1)
    cls = place & 3
    high = cls >= 2
    odd = (cls & 1) == 1
    low_lane = lane < 64
    heads = [jnp.where(high, block[:, 128:256], block[:, 0:128]) for block in columns]

    def pair(left, right):
        moved = pltpu.roll(jnp.where(odd, left, right), 64, 1)
        return jnp.where(low_lane == odd, moved, jnp.where(odd, right, left))

    picked = [pair(heads[0], heads[1])]
    if turn == 0:
        step = (place >> 2) & 3
        sorted_at = cls * 256 + (((step & 1) << 1) | (step >> 1)) * 64 + (place >> 4)
        ids = jnp.where(lane == 64, sorted_at >> 7, jnp.where(lane == 65, sorted_at & 127, 0)).astype(F32)
        q = heads[2] * 0.125
        picked.append(jnp.where(low_lane, jnp.where(odd, pltpu.roll(q, 64, 1), q), ids))
    if turn == 1:
        picked.append(pair(heads[2] * 0.125, heads[3] * 0.125))
        picked.append(pair(heads[4], heads[5]))
    return picked


ARRIVAL = (0, 2, 1, 3)
PAIR_OF = ((0, 1), (2, 3), (1, 0))
LN2 = (0.69140625, 0.0017409306)
LN3 = (1.1015625, -0.0029502113)

def key_table(group, inner):
    lane = iota((128, 128), 1)
    key = iota((128, 128), 0) // 64 + 2 * (group % 2)
    third, second = PAIR_OF[group]
    query = jnp.where(lane < 69, lane - 65, lane - 69)
    used = (lane >= 65) & (lane < 73)
    twice = used & ((query == third) | (query == second))
    thrice = used & (query == third) & (key == third)
    first = lane < 69
    ln2 = jnp.where(first, LN2[0], LN2[1])
    ln3 = jnp.where(first, LN3[0], LN3[1])
    if inner:
        return jnp.where(thrice, ln3, jnp.where(twice, ln2, 0.0))
    return jnp.where(thrice, ln2, 0.0)


def layer_kernel(
    tiles, dest, w_in, gain, w_qkv, valid, back,
    tiles_v, w_in_v, w_qkv_v, dest_v, gain_v, normed_v, out0, out1, in0, in1, hot,
    own, sib, x_own, x_sib, stage, q_op, k_op, v_op, xk_op, xv_op, tops, sums, attn, q_tab, k_tab, x_tab,
    load_sem, go_sem, come_sem, stay_sem,
    send_sem, recv_sem, sib_send, sib_recv, x_send, x_recv, xs_send, xs_recv, out_send, out_recv, own_sem,
):
    slide = lax.axis_index("slide")
    seq = lax.axis_index("seq")
    me = slide * SEQ + seq
    across = seq // PLACES
    place_me = lax.rem(seq, PLACES)
    half = seq // 8
    row = lax.rem(seq // 4, 2)
    col = lax.rem(seq // 2, 2)
    core = lax.rem(seq, 2)
    leaving, coming = (out0, out1), (in0, in1)

    def place_at(step):
        return lax.rem(place_me + step, PLACES)

    loads = [
        pltpu.make_async_copy(w_in, w_in_v, load_sem.at[0]),
        pltpu.make_async_copy(w_qkv, w_qkv_v, load_sem.at[1]),
        pltpu.make_async_copy(dest, dest_v, load_sem.at[2]),
        pltpu.make_async_copy(gain, gain_v, load_sem.at[3]),
    ]
    for step in range(PLACES):
        loads.append(pltpu.make_async_copy(tiles.at[:, place_at(step)], tiles_v.at[step], load_sem.at[4 + step]))
    for index in (0, 4, 2, 3, 1, 5, 6, 7):
        loads[index].start()

    barrier = pltpu.get_barrier_semaphore()

    @pl.loop(1, DEVICES)
    def _(i):
        other = lax.rem(me + i, DEVICES)
        pl.semaphore_signal(barrier, inc=1, device_id=(other // SEQ, lax.rem(other, SEQ)), device_id_type=MESH)

    def project(step):
        x = tiles_v[step].reshape(CHUNK, E)
        proj = jnp.dot(x, w_in_v[...], preferred_element_type=F32).astype(BF).astype(F32)
        mean = jnp.mean(proj, axis=-1, keepdims=True)
        centred = proj - mean
        var = jnp.mean(centred * centred, axis=-1, keepdims=True)
        gains = jnp.concatenate([gain_v[i : i + 1, :] for i in range(D // 128)], axis=1)
        normed_v[step] = (centred * lax.rsqrt(var + 1e-05) * gains).astype(BF)

    def fill(step, turn):
        place = place_at(step)
        normed = normed_v[step]
        columns = [
            jnp.dot(normed, w_qkv_v[:, kind * D + group * 256 : kind * D + group * 256 + 256], preferred_element_type=F32)
            for kind, group in NEEDS[turn]
        ]
        lines = (dest_v[...] & (ROWS - 1)).astype(F32)
        lines = jnp.broadcast_to(lines.reshape(8, 1, 128), (8, 32, 128)).reshape(CHUNK, 128)
        r = iota((CHUNK, 128), 0)
        wanted = ((r >> 3) & 3) * 32 + place * 8 + (r & 7)
        position = jnp.sum(jnp.where(iota((CHUNK, 128), 1) == wanted, lines, 0.0), axis=1, keepdims=True).astype(I32)
        for index, block in enumerate(pick_columns(turn, columns, position)):
            lanes = pl.ds(index * 128, 128)
            leaving[turn][:, place, :, lanes] = block.reshape(CHUNK // BLOCK, BLOCK, 128).astype(BF)

    def leave(step, turn):
        place = place_at(step)

        @pl.loop(1 if step == 0 else 0, CHUNK // BLOCK)
        def _(i):
            to_slide = lax.rem(slide + i, SLIDES)
            to_across = lax.rem(across + i // SLIDES, 4)
            pltpu.make_async_remote_copy(
                src_ref=leaving[turn].at[to_slide * 4 + to_across, place],
                dst_ref=coming[turn].at[me],
                send_sem=go_sem.at[turn],
                recv_sem=come_sem.at[turn],
                device_id=(to_slide, to_across * PLACES + place),
                device_id_type=MESH,
            ).start()

    def stay(turn):
        copy = pltpu.make_async_copy(
            leaving[turn].at[slide * 4 + across, place_me], coming[turn].at[me], stay_sem.at[turn]
        )
        copy.start()
        copy.wait()

    others = pl.ds(0, DEVICES - 1)

    def arrived(turn):
        part = coming[turn].at[others]
        pltpu.make_async_copy(part, part, come_sem.at[turn]).wait()

    def left(turn):
        part = coming[turn].at[others]
        pltpu.make_async_copy(part, part, go_sem.at[turn]).wait()

    def slot(d):
        return 2 * lax.rem(row + d // 2, 2) + lax.rem(col + d % 2, 2)

    def cross_slot(d):
        return 2 * lax.rem(1 - row + d // 2, 2) + lax.rem(col + d % 2, 2)

    def cls_of(d):
        return 2 * lax.rem(row + d // 2 + half, 2) + lax.rem(col + d % 2, 2)

    def device(d):
        return (slide, half * 8 + slot(d) * 2 + core)

    sibling = (slide, seq + 1 - 2 * core)
    cross = (slide, (1 - half) * 8 + cross_slot(0) * 2 + core)

    low64 = iota((64, 128), 1) < 64

    def target(d):
        return own.at[0] if d == 0 else stage.at[d - 1]

    def mark():
        lane8 = iota((8, 128), 1)
        weigh = jnp.where(lane8 == 64, 128.0, jnp.where(lane8 == 65, 1.0, 0.0)).astype(BF)
        ids = in0[...].reshape(ROWS, WIDTHS[0])[:, 128:256]
        at = lax.dot_general(weigh, ids, (((1,), (1,)), ((), ())), preferred_element_type=F32)
        at = at[0:1].astype(I32)
        for d in range(4):
            hit = (at - cls_of(d) * 256) == iota((256, ROWS), 0)
            hot[d] = jnp.where(hit, 1.0, 0.0).astype(BF)

    def sort(d, turn):
        rows_in = coming[turn][...].reshape(ROWS, WIDTHS[turn])
        found = jnp.dot(hot[d], rows_in, preferred_element_type=F32)
        ref = target(d)

        def tile(a, t):
            return found[a * 64 : a * 64 + 64, t * 128 : t * 128 + 128]

        for group, at_tile in ((0, 0),) if turn == 0 else ((1, 0), (2, 2)):
            for i in range(4):
                ref[6 * group + i] = tile((2 * (group % 2) + i) % 4, at_tile).astype(BF)
        for pair in range(2):
            even, odd = tile(2 * pair, 1), tile(2 * pair + 1, 1)
            ref[6 * turn + 4 + pair] = jnp.where(low64, even, pltpu.roll(odd, 64, 1)).astype(BF)
            if turn == 1:
                ref[16 + pair] = jnp.where(low64, pltpu.roll(even, 64, 1), odd).astype(BF)

    def remote(src, dst, send, recv_, to):
        return pltpu.make_async_remote_copy(
            src_ref=src, dst_ref=dst, send_sem=send, recv_sem=recv_, device_id=to, device_id_type=MESH
        )

    sends = {}

    def send(d, group):
        part = pl.ds(6 * group, 6)
        copy = remote(
            stage.at[d - 1, part], own.at[d, part], send_sem.at[d - 1, group], recv_sem.at[d - 1, group], device(d)
        )
        copy.start()
        sends[d, group] = copy

    sib_copies, x_copies, xs_copies = {}, {}, {}

    def share(d, group):
        if d > 0:
            sends[d, group].wait_recv()
        sib_copies[d, group] = remote(
            own.at[d, pl.ds(6 * group, 4)], sib.at[d, pl.ds(4 * group, 4)], sib_send.at[d, group], sib_recv.at[d, group], sibling
        )
        sib_copies[d, group].start()
        x_copies[d, group] = remote(
            own.at[d, pl.ds(6 * group, 2)], x_own.at[d, pl.ds(2 * group, 2)], x_send.at[d, group], x_recv.at[d, group], cross
        )
        x_copies[d, group].start()

    def share_cross(d, group):
        x_copies[d, group].wait_recv()
        part = pl.ds(2 * group, 2)
        xs_copies[d, group] = remote(x_own.at[d, part], x_sib.at[d, part], xs_send.at[d, group], xs_recv.at[d, group], sibling)
        xs_copies[d, group].start()

    cls = cls_of(0)
    length = valid[slide]
    lane = iota((128, 128), 1)
    low_lane = lane < 64
    line = iota((128, 128), 0)
    steps = lax.rem(line, 64) * 16 + (line // 64) * 8

    def start_of(half_, slot_, core_):
        return half_ * 8192 + slot_ * 2048 + core_ * 1024 + cls

    for pair in range(2):
        residue = line // 64 + 2 * pair
        ones = jnp.where((lane == 64) | (lane == 65 + residue) | (lane == 69 + residue), 1.0, 0.0)
        q_tab[pair] = ones.astype(BF)
    for group in range(3):
        k_tab[group] = key_table(group, True).astype(BF)
        x_tab[group] = key_table(group, False).astype(BF)

    def keys(k_ref, v_ref, group, at_row, block, position, table):
        block = block.reshape(128, 128)
        bias = jnp.where((lane == 64) & (position >= length), jnp.full_like(block, -1e30), table)
        k_ref[group, at_row : at_row + 128, :] = jnp.where(low_lane, block, bias)
        v_ref[group, at_row : at_row + 128, :] = jnp.where(low_lane, jnp.ones_like(block), block)

    def prepare(e, group):
        d = ARRIVAL[e]
        for pair in range(2):
            packed = own[d, 6 * group + 4 + pair].astype(F32)
            q = jnp.concatenate([packed, pltpu.roll(packed, 64, 1)], axis=0).astype(BF)
            begin = e * 256 + pair * 128
            q_op[group, begin : begin + 128, :] = jnp.where(low_lane, q, q_tab[pair])
        sib_copies[d, group].wait_recv()
        for source, core_, first in ((own, core, 6 * group), (sib, 1 - core, 4 * group)):
            for rest in range(2):
                at_row = e * 512 + rest * 256 + (0 if source is own else 128)
                position = steps + (start_of(half, slot(d), core_) + 4 * ((group + rest) % 2))
                table = k_tab[group] if rest == 0 else jnp.zeros((128, 128), BF)
                at_tile = first + 2 * rest
                keys(k_op, v_op, group, at_row, source[d, at_tile : at_tile + 2], position, table)

    def prepare_cross(e, group):
        d = ARRIVAL[e]
        xs_copies[d, group].wait_recv()
        for source, core_ in ((x_own, core), (x_sib, 1 - core)):
            at_row = e * 256 + (0 if source is x_own else 128)
            position = steps + (start_of(1 - half, cross_slot(d), core_) + 4 * (group % 2))
            keys(xk_op, xv_op, group, at_row, source[d, 2 * group : 2 * group + 2], position, x_tab[group])

    contract = (((1,), (1,)), ((), ()))

    def mix(q, k_ref, v_ref, group, spans, state):
        for begin, end in spans:
            span = pl.ds(begin, end - begin)
            scores = lax.dot_general(q, k_ref[group, span, :], contract, preferred_element_type=F32)
            top = jnp.broadcast_to(jnp.max(scores, axis=1, keepdims=True), (q.shape[0], 128))
            if state is not None:
                top = jnp.maximum(state[0], top)
            expo = jnp.exp(scores - jnp.concatenate([top] * ((end - begin) // 128), axis=1)).astype(BF)
            acc = jnp.dot(expo, v_ref[group, span, :], preferred_element_type=F32)
            if state is not None:
                acc += state[1] * jnp.exp(state[0] - top)
            state = (top, acc)
        return state

    outs = []

    def give(e, group, pair):
        d = ARRIVAL[e]
        acc = sums[group, e * 256 + pair * 128 : e * 256 + pair * 128 + 128, :]
        position = steps + (start_of(half, slot(d), core) + 4 * pair)
        out = jnp.where(position < length, acc / pltpu.roll(acc, 64, 1), 0.0)
        attn[d, 2 * group + pair] = jnp.where(low64, pltpu.roll(out[0:64], 64, 1), out[64:128]).astype(BF)
        src, dst = attn.at[d, 2 * group + pair], back.at[cls, 2 * group + pair]
        if d > 0:
            copy = remote(src, dst, out_send.at[2 * group + pair, d - 1], out_recv.at[2 * group + pair, d - 1], device(d))
        else:
            copy = pltpu.make_async_copy(src, dst, own_sem.at[2 * group + pair])
        copy.start()
        outs.append(copy)

    def attend_half(group):
        for e in range(4):
            prepare(e, group)
        spans = [(begin, begin + 512) for begin in range(0, 2048, 512)]
        tops[group], sums[group] = mix(q_op[group], k_op, v_op, group, spans, None)
        for e in (3, 1, 2, 0):
            give(e, group, 1 - group % 2)

    def attend_cross(groups):
        found = []
        for group in groups:
            first = 128 * (group % 2)
            rows = [pl.ds(e * 256 + first, 128) for e in range(4)]
            q, top, acc = [jnp.concatenate([ref[group, r, :] for r in rows], axis=0) for ref in (q_op, tops, sums)]
            found.append((group, rows, mix(q, xk_op, xv_op, group, ((0, 512), (512, 1024)), (top, acc))[1]))
        for group, rows, acc in found:
            for e in range(4):
                sums[group, rows[e], :] = acc[e * 128 : e * 128 + 128]
        for group in groups:
            for e in (3, 1, 2, 0):
                give(e, group, group % 2)

    def exchange(turn):
        stay(turn)
        arrived(turn)
        if turn == 0:
            mark()
        for d in ARRIVAL[1:]:
            sort(d, turn)
            send(d, turn)
        if turn == 1:
            for d in ARRIVAL[1:]:
                send(d, 2)
        sort(0, turn)
        for group in (0,) if turn == 0 else (1, 2):
            share(0, group)

    for index in (0, 3, 4):
        loads[index].wait()
    project(0)
    for index in (1, 2):
        loads[index].wait()
    for step in range(PLACES):
        if step + 1 < PLACES:
            loads[5 + step].wait()
            project(step + 1)
        fill(step, 0)
        if step == 1:
            pl.semaphore_wait(barrier, DEVICES - 1)
            leave(0, 0)
        if step >= 1:
            leave(step, 0)
    for step in range(PLACES):
        fill(step, 1)
        leave(step, 1)
    exchange(0)
    exchange(1)
    for d in ARRIVAL[1:]:
        share(d, 0)
    attend_half(0)
    for d in ARRIVAL[1:]:
        share(d, 1)
    for d in ARRIVAL:
        share_cross(d, 0)
    attend_half(1)
    for d in ARRIVAL[1:]:
        share(d, 2)
    for d in ARRIVAL:
        share_cross(d, 1)
    for group in range(2):
        for e in range(4):
            prepare_cross(e, group)
    attend_cross((0, 1))
    for d in ARRIVAL:
        share_cross(d, 2)
    attend_half(2)
    for e in range(4):
        prepare_cross(e, 2)
    attend_cross((2,))
    for copy in outs:
        copy.wait()
    for turn in range(2):
        left(turn)
    for group in range(3):
        for d in range(4):
            if d > 0:
                sends[d, group].wait_send()
            sib_copies[d, group].wait_send()
            x_copies[d, group].wait_send()
            xs_copies[d, group].wait_send()


def layer(tiles, dest, w_in, gain, w_qkv, valid):
    hbm = pl.BlockSpec(memory_space=pltpu.HBM)
    dma = pltpu.SemaphoreType.DMA
    blocks = DEVICES // PLACES
    return pl.pallas_call(
        layer_kernel,
        out_shape=jax.ShapeDtypeStruct((4, 6, 64, 128), BF),
        in_specs=[hbm] * 5 + [pl.BlockSpec(memory_space=pltpu.SMEM)],
        out_specs=hbm,
        scratch_shapes=[
            pltpu.VMEM((PLACES, blocks, BLOCK, E), BF),
            pltpu.VMEM((E, D), BF),
            pltpu.VMEM((D, 3 * D), BF),
            pltpu.VMEM((8, 128), I32),
            pltpu.VMEM((D // 128, 128), F32),
            pltpu.VMEM((PLACES, CHUNK, D), BF),
            *[pltpu.VMEM((blocks, PLACES, BLOCK, width), BF) for width in WIDTHS],
            *[pltpu.VMEM((DEVICES, BLOCK, width), BF) for width in WIDTHS],
            pltpu.VMEM((4, 256, ROWS), BF),
            pltpu.VMEM((4, 18, 64, 128), BF),
            pltpu.VMEM((4, 12, 64, 128), BF),
            pltpu.VMEM((4, 6, 64, 128), BF),
            pltpu.VMEM((4, 6, 64, 128), BF),
            pltpu.VMEM((3, 18, 64, 128), BF),
            pltpu.VMEM((3, 1024, 128), BF),
            pltpu.VMEM((3, 2048, 128), BF),
            pltpu.VMEM((3, 2048, 128), BF),
            pltpu.VMEM((3, 1024, 128), BF),
            pltpu.VMEM((3, 1024, 128), BF),
            pltpu.VMEM((3, 1024, 128), F32),
            pltpu.VMEM((3, 1024, 128), F32),
            pltpu.VMEM((4, 6, 64, 128), BF),
            pltpu.VMEM((2, 128, 128), BF),
            pltpu.VMEM((3, 128, 128), BF),
            pltpu.VMEM((3, 128, 128), BF),
            dma((4 + PLACES,)),
            dma((3,)),
            dma((3,)),
            dma((3,)),
            dma((3, 3)),
            dma((3, 3)),
            *[dma((4, 3)) for _ in range(6)],
            dma((6, 3)),
            dma((6, 3)),
            dma((6,)),
        ],
        compiler_params=pltpu.CompilerParams(collective_id=0, has_side_effects=True, vmem_limit_bytes=VMEM_LIMIT),
        name="layer",
    )(tiles, dest, w_in, gain, w_qkv, valid)


def output_kernel(rows_hbm, weight_hbm, out, rows_in, weight, spread, packed, load_sem, out_sem):
    loads = [pltpu.make_async_copy(rows_hbm, rows_in, load_sem.at[0])]
    for part in range(2):
        lanes = pl.ds(part * (D // 2), D // 2)
        loads.append(pltpu.make_async_copy(weight_hbm.at[:, lanes], weight.at[part], load_sem.at[1 + part]))
    for copy in loads:
        copy.start()
    loads[0].wait()
    low = iota((64, 128), 1) < 64
    rows = []
    for cls in range(4):
        columns = []
        for g in range(3):
            tiles = [rows_in[cls, 2 * g + a // 2] for a in range(4)]
            masked = [jnp.where(low == (a % 2 == 0), tile, jnp.zeros_like(tile)) for a, tile in enumerate(tiles)]
            columns.append(jnp.concatenate(masked, axis=0))
        rows.append(jnp.concatenate(columns, axis=1))
    copies = []
    for part in range(2):
        loads[1 + part].wait()
        for cls in range(4):
            heads = [weight[part, (cls + 4 * g) * 64 : (cls + 4 * g + 1) * 64, :] for g in range(3)]
            wide = jnp.concatenate([w for w in heads for _ in range(2)], axis=0)
            total = jnp.dot(rows[cls], wide, preferred_element_type=F32)
            for a in range(4):
                residue = cls + (a % 2) * 8 + (a // 2) * 4
                for t in range(3):
                    spread[3 * part + t, pl.ds(residue, 64, stride=16), :] = total[a * 64 : a * 64 + 64, t * 128 : t * 128 + 128]
        for t in range(3):
            packed[part, :, t * 128 : t * 128 + 128] = spread[3 * part + t].astype(BF)
        copy = pltpu.make_async_copy(packed.at[part], out.at[:, pl.ds(part * (D // 2), D // 2)], out_sem.at[part])
        copy.start()
        copies.append(copy)
    for copy in copies:
        copy.wait()


def output(rows_in, weight):
    hbm = pl.BlockSpec(memory_space=pltpu.HBM)
    return pl.pallas_call(
        output_kernel,
        out_shape=jax.ShapeDtypeStruct((ROWS, D), BF),
        in_specs=[hbm, hbm],
        out_specs=hbm,
        scratch_shapes=[
            pltpu.VMEM((4, 6, 64, 128), BF),
            pltpu.VMEM((2, D, D // 2), BF),
            pltpu.VMEM((D // 128, ROWS, 128), F32),
            pltpu.VMEM((2, ROWS, D // 2), BF),
            pltpu.SemaphoreType.DMA((3,)),
            pltpu.SemaphoreType.DMA((2,)),
        ],
        compiler_params=pltpu.CompilerParams(vmem_limit_bytes=VMEM_LIMIT),
        name="output",
    )(rows_in, weight)


def local(tiles, destination, valid_len, in_weight, norm_gain, qkv_weight, out_weight):
    blocks = DEVICES // PLACES
    back = layer(
        tiles.reshape(blocks, PLACES, BLOCK, E),
        destination.reshape(8, 128),
        in_weight,
        norm_gain.reshape(D // 128, 128),
        qkv_weight,
        valid_len,
    )
    return output(back, out_weight).reshape(1, ROWS, D)


def solution(mesh):
    in_specs = (P(("slide", "seq"), None), P(("slide", "seq")), P(), P(), P(), P(), P())
    return jax.shard_map(local, mesh=mesh, in_specs=in_specs, out_specs=P("slide", "seq", None), check_vma=False)
```
